256 devices in a mesh: gx: 16 (over z, y_lo), gy: 16 (over x, y_hi, core).
Axes of the slice: x: 4, y: 4 (y_hi: 2, y_lo: 2; y = y_hi * 2 + y_lo), z: 8, core: 2. Of those that a mesh axis runs over, the one named last changes fastest.
Arguments:
- field_slab: bfloat16 [1536, 256, 64], P('gx', 'gy'), may hold values from -6 to 6
- one_by_second: bfloat16 [256, 400], P('gy'), may hold values from -0.375 to 0.375
- one_by_hours: bfloat16 [64, 400], replicated, may hold values from -0.75 to 0.75
- two_by_first: bfloat16 [1536, 400], P('gx'), may hold values from -0.15625 to 0.15625
- two_by_hours: bfloat16 [64, 400], replicated, may hold values from -0.75 to 0.75
- three_by_first: bfloat16 [1536, 400], P('gx'), may hold values from -0.15625 to 0.15625
- three_by_second: bfloat16 [256, 400], P('gy'), may hold values from -0.375 to 0.375
- core_first: bfloat16 [800, 1536], P(None, 'gx'), may hold values from -0.15625 to 0.15625
- core_second: bfloat16 [800, 256], P(None, 'gy'), may hold values from -0.375 to 0.375
- core_hours: bfloat16 [800, 64], replicated, may hold values from -0.75 to 0.75
Outputs:
- mode_one: float32 [1536, 400], P(('gx', 'gy'))
- mode_two: float32 [256, 400], P('gy')
- mode_three: float32 [64, 400], replicated
- core_sketch: float32 [800, 800, 800], P('gx', 'gy')
The draws below stay inside these ranges and needn't reach their ends.
All inputs are finite; a program needn't handle non-finite values.
Results may differ from the reference program's by a relative error of at most 0.0041.
Values may be sent and summed in bfloat16 or wider, within the bound.
A program may use at most 64 MiB of HBM per device.

```python
import jax
import jax.numpy as jnp
from jax import lax

CX = 96
HOURS = 64
K = 400
S = 800
NX = 1536
NY = 256
N_GX = 16


def block_scale(rng, extent, split, least, high):
    level, own = 1.0, jax.random.fold_in(rng, 6)
    for dim, blocks in split:
        heights = jnp.exp(jax.random.uniform(jax.random.fold_in(own, dim), (blocks,), jnp.float32, least / len(split), high / len(split)))
        level = level * jnp.repeat(heights, extent[dim] // blocks).reshape([-1 if axis == dim else 1 for axis in range(len(extent))])
    return level


def gaussian(own_key, extent, spread, reach, split=(), dtype=jnp.bfloat16):
    array = jax.random.normal(own_key, extent, jnp.float32) * spread
    if len(split) > 0:
        array = block_scale(own_key, extent, split, -0.22, 0.18) * array
    return jnp.clip(array, min=-reach, max=reach).astype(dtype)


def setup_inputs(seed: int = 0) -> dict:
    keys = jax.random.split(jax.random.key(seed), 11)
    return {
        "field_slab": gaussian(keys[0], (NX, NY, HOURS), 1.0, 6.0, ((0, 16), (1, 16))),
        "one_by_second": gaussian(keys[1], (NY, K), NY ** -0.5, 0.375, ((0, 16),)),
        "one_by_hours": gaussian(keys[2], (HOURS, K), HOURS ** -0.5, 0.75),
        "two_by_first": gaussian(keys[3], (NX, K), NX ** -0.5, 0.15625, ((0, 16),)),
        "two_by_hours": gaussian(keys[4], (HOURS, K), HOURS ** -0.5, 0.75),
        "three_by_first": gaussian(keys[5], (NX, K), NX ** -0.5, 0.15625, ((0, 16),)),
        "three_by_second": gaussian(keys[6], (NY, K), NY ** -0.5, 0.375, ((0, 16),)),
        "core_first": gaussian(keys[7], (S, NX), NX ** -0.5, 0.15625, ((1, 16),)),
        "core_second": gaussian(keys[8], (S, NY), NY ** -0.5, 0.375, ((1, 16),)),
        "core_hours": gaussian(keys[9], (S, HOURS), HOURS ** -0.5, 0.75),
    }


def reference(field_slab, one_by_second, one_by_hours, two_by_first, two_by_hours, three_by_first, three_by_second, core_first, core_second, core_hours):
    flat_field = field_slab.reshape(NX, NY * HOURS)
    test_one = (one_by_second.astype(jnp.float32)[:, None, :] * one_by_hours.astype(jnp.float32)[None, :, :]).astype(jnp.bfloat16).reshape(NY * HOURS, K)
    mode_one = jnp.dot(flat_field, test_one, preferred_element_type=jnp.float32)
    test_two = (two_by_first.astype(jnp.float32)[:, None, :] * two_by_hours.astype(jnp.float32)[None, :, :]).astype(jnp.bfloat16).reshape(NX * HOURS, K)
    turned = jnp.transpose(field_slab, (1, 0, 2)).reshape(NY, NX * HOURS)
    mode_two = jnp.dot(turned, test_two, preferred_element_type=jnp.float32)

    def hour_block(block_index, summed):
        offset = (block_index * CX).astype(jnp.int32)
        row_block = lax.dynamic_slice_in_dim(field_slab, offset, CX, 0)
        first_rows = lax.dynamic_slice_in_dim(three_by_first, offset, CX, 0)
        test_three = (first_rows.astype(jnp.float32)[:, None, :] * three_by_second.astype(jnp.float32)[None, :, :]).astype(jnp.bfloat16).reshape(CX * NY, K)
        return summed + lax.dot_general(row_block.reshape(CX * NY, HOURS), test_three, (((0,), (0,)), ((), ())), preferred_element_type=jnp.float32)

    mode_three = lax.fori_loop(jnp.int32(0), jnp.int32(N_GX), hour_block, jnp.zeros((HOURS, K), jnp.float32))
    first_mode = jnp.dot(core_first, flat_field, preferred_element_type=jnp.float32).astype(jnp.bfloat16).reshape(S, NY, HOURS)
    second_mode = jnp.einsum('bj,ajt->bat', core_second.astype(jnp.float32), first_mode.astype(jnp.float32)).astype(jnp.bfloat16)
    core_sketch = jnp.einsum('bat,ct->abc', second_mode.astype(jnp.float32), core_hours.astype(jnp.float32))
    return mode_one, mode_two, mode_three, core_sketch
```

```python
import jax
import jax.numpy as jnp
from jax import lax
from jax.experimental import pallas as pl
from jax.experimental.pallas import tpu as pltpu
from jax.sharding import PartitionSpec as P

MESH = pl.DeviceIdType.MESH
F32 = jnp.float32
BF16 = jnp.bfloat16
N = 16
NZ = 8
WIN = 512
BLK = 64
OFFSETS = (0, -1, 1, -2, 2, -3, 3, -4)


def exchange_kernel(
    f_ref, cf_ref, c2_ref, s1_ref, h1_ref, f2_ref, h2_ref, f3_ref, s3_ref,
    rr_out, m1_out, m23_out,
    f32s, fblk, fall, cfall, c2f, c2all, s1f, s3f, acc, acct, fms, fmr, lhsf, sms, rr,
    m1a, m2a, m3a, m1s, m1r, g1s, g1r, g2s, g2r, g3s, g3r,
    fs, fr, ffs, ffr, zs, zr, ys, yr, cs, cr, p2s, p2r, p3s, p3r,
    m1ss, m1rs, g1ss, g1rs, g2ss, g2rs, g3ss, g3rs,
):
    mx, my = lax.axis_index("gx"), lax.axis_index("gy")
    core = lax.rem(my, 2)
    place = my // 2
    ylo, z = lax.rem(mx, 2), mx // 2
    yhi, x = lax.rem(place, 2), place // 2
    other = (mx, my + 1 - 2 * core)
    y = 2 * yhi + ylo

    def at_y(there):
        there = lax.rem(there, 4)
        return (2 * z + lax.rem(there, 2), 4 * x + 2 * (there // 2) + core)

    y_up, y_down = at_y(y + 1), at_y(y + 3)
    z_up = (2 * lax.rem(z + 1, NZ) + ylo, my)
    z_down = (2 * lax.rem(z + NZ - 1, NZ) + ylo, my)

    def send(src, dst, send_sem, recv_sem, device):
        return pltpu.make_async_remote_copy(
            src_ref=src, dst_ref=dst, send_sem=send_sem, recv_sem=recv_sem,
            device_id=device, device_id_type=MESH,
        )

    def gx_peer(r):
        return lax.rem(mx + r, N)

    def gy_peer(r):
        return lax.rem(my + r, N)

    def each(low, high, body):
        def step(i, carry):
            body(i)
            return carry

        lax.fori_loop(low, high, step, 0)

    barrier = pltpu.get_barrier_semaphore()

    def greet(r):
        pl.semaphore_signal(barrier, inc=1, device_id=(gx_peer(r), my), device_id_type=MESH)
        pl.semaphore_signal(barrier, inc=1, device_id=(mx, gy_peer(r)), device_id_type=MESH)

    each(1, N, greet)
    across = (mx + 1 - 2 * ylo, my + 2 - 4 * yhi)
    pl.semaphore_signal(barrier, inc=1, device_id=across, device_id_type=MESH)
    half = mx // 8
    same = jnp.logical_and(mx == my, half == core)

    def greet_turned(s):
        @pl.when(jnp.logical_not(jnp.logical_and(my == mx, 2 * s + half == my)))
        def _():
            pl.semaphore_signal(
                barrier, inc=1, device_id=(my, 2 * s + half), device_id_type=MESH
            )

    each(0, 8, greet_turned)

    for j in range(16):
        f32s[64 * j : 64 * j + 64, 0:96] = f_ref[j].astype(F32)
    for t in range(64):
        fblk[t // 4, t % 4] = f32s[pl.ds(t, 16, stride=64), :][:, 0:96].astype(BF16)

    cfall[mx, :, 384:512] = jnp.zeros((96, 128), BF16)

    @pl.when(core == 0)
    def _():
        cfall[mx] = cf_ref[:, 0:512]

    @pl.when(core == 1)
    def _():
        cfall[mx, :, 0:416] = cf_ref[:, 384:800]

    c2f[...] = jnp.zeros_like(c2f)
    for g in range(N):
        c2f[:, BLK * g : BLK * g + 50] = c2_ref[:, 50 * g : 50 * g + 50].astype(F32)
    c2all[place, core] = c2f[...].astype(BF16)

    pl.semaphore_wait(barrier, 2 * (N - 1) + 1 + 8 - same.astype(jnp.int32))

    def shard(o, low):
        return 2 * lax.rem(z + o + NZ, NZ) + low

    def z_copy(direction, step):
        o = -direction * (step - 1)
        index = step - 1 if direction > 0 else 3 + step
        slot = cfall.at[shard(o, ylo)]
        return send(slot, slot, zs.at[index], zr.at[index], z_up if direction > 0 else z_down)

    def y_copy(o, h):
        slot = cfall.at[shard(o, ylo), pl.ds(48 * h, 48)]
        index = 2 * (o + 4) + h
        return send(slot, slot, ys.at[index], yr.at[index], y_up if h == 0 else y_down)

    def pass_on(o):
        y_copy(o, 0).start()
        y_copy(o, 1).start()

    def ring(step):
        z_copy(1, step).wait_recv()
        if step < 4:
            z_copy(1, step + 1).start()
        if step < 4:
            z_copy(-1, step).wait_recv()
            if step < 3:
                z_copy(-1, step + 1).start()
        pass_on(-step)
        if step < 4:
            pass_on(step)

    def f_copy(r):
        return send(
            fblk.at[gx_peer(r)], fall.at[mx, :, core], fs.at[r], fr.at[r], (gx_peer(r), my)
        )

    def f_forward(r):
        slot = fall.at[lax.rem(mx + N - r, N), :, core]
        return send(slot, slot, ffs.at[r], ffr.at[r], other)

    z_copy(1, 1).start()
    z_copy(-1, 1).start()
    pass_on(0)
    each(1, N, lambda r: f_copy(r).start())
    for t in range(4):
        fall[mx, t, core] = fblk[mx, t]
    f_forward(0).start()

    c2_y = send(
        c2all.at[place, core], c2all.at[place, core], cs.at[0], cr.at[0],
        (mx, my + 2 - 4 * yhi),
    )
    c2_y.start()

    def c2_x(r):
        pair = c2all.at[pl.ds(2 * x, 2), core]
        return send(
            pair, pair, cs.at[r], cr.at[r], (mx, 4 * lax.rem(x + r, 4) + 2 * yhi + core)
        )

    mine = c2all.at[:, core]
    c2_core = send(mine, mine, cs.at[4], cr.at[4], other)

    s1f[...] = s1_ref[...].astype(F32)
    s3f[...] = s3_ref[...].astype(F32)
    m1a[...] = jnp.zeros_like(m1a)
    m3a[...] = jnp.zeros_like(m3a)
    m1s[...] = jnp.zeros_like(m1s)
    g1s[...] = jnp.zeros_like(g1s)

    def modes(low, high):
        def one(j):
            rows = f_ref[j]
            turned = (((0,), (0,)), ((), ()))
            by_one = lax.dot_general(rows, h1_ref[...], turned, preferred_element_type=F32)
            m1a[...] += by_one * s1f[pl.ds(j, 1), :]
            by_two = lax.dot_general(rows, h2_ref[...], turned, preferred_element_type=F32)
            m2a[pl.ds(j, 1), :] = jnp.sum(by_two * f2_ref[...].astype(F32), axis=0, keepdims=True)
            by_three = jnp.dot(rows, f3_ref[...], preferred_element_type=F32)
            m3a[...] += by_three * s3f[pl.ds(j, 1), :]

        each(low, high, one)

    modes(0, 5)
    ring(1)
    modes(5, 10)
    c2_y.wait_recv()
    each(1, 4, lambda r: c2_x(r).start())
    ring(2)
    modes(10, 16)
    ring(3)

    def field_arrives(r):
        f_copy(r).wait_recv()
        f_forward(r).start()

    each(1, N, field_arrives)
    ring(4)

    for g in range(N):
        g1s[g, 0:4] = m3a[4 * g : 4 * g + 4]
        g1s[g, 4:5] = m2a[g : g + 1]
        m1s[g, 0:6] = m1a[6 * g : 6 * g + 6]

    def g1_copy(r):
        return send(g1s.at[gx_peer(r)], g1r.at[mx], g1ss.at[r], g1rs.at[r], (gx_peer(r), my))

    def m1_copy(r):
        return send(m1s.at[gy_peer(r)], m1r.at[my], m1ss.at[r], m1rs.at[r], (mx, gy_peer(r)))

    def g2_copy(r):
        return send(g2s, g2r.at[my], g2ss.at[r], g2rs.at[r], (mx, gy_peer(r)))

    def g3_copy(r):
        return send(g3s, g3r.at[mx], g3ss.at[r], g3rs.at[r], (gx_peer(r), my))

    each(1, N, lambda r: g1_copy(r).start())
    g1r[mx] = g1s[mx]
    m1r[my] = m1s[my]

    each(1, 4, lambda r: c2_x(r).wait_recv())
    c2_core.start()
    each(0, N, lambda r: f_forward(r).wait_recv())

    def add_shard(g):
        acc[...] += jnp.dot(fall[g].reshape(128, 96), cfall[g], preferred_element_type=F32)

    acc[...] = jnp.zeros_like(acc)
    for o in OFFSETS:
        add_shard(shard(o, ylo))
        y_copy(o, 0).wait_recv()
        y_copy(o, 1).wait_recv()
        add_shard(shard(o, 1 - ylo))
    acct[...] = acc[...].T

    def m_copy(m):
        return send(fms.at[m], fmr.at[place], p2s.at[m], p2r.at[place], (8 * core + m, mx))

    def not_self(m):
        return jnp.logical_not(jnp.logical_and(8 * core + m == mx, mx == my))

    for m in range(8):
        fms[m] = acct[pl.ds(16 * core + 50 * m, BLK), :].astype(BF16)

        @pl.when(not_self(m))
        def _():
            m_copy(m).start()

        @pl.when(jnp.logical_not(not_self(m)))
        def _():
            fmr[place] = fms[m]

    each(1, N, lambda r: m1_copy(r).start())

    each(1, N, lambda r: g1_copy(r).wait_recv())
    g2s[...] = jnp.sum(g1r[...], axis=0)
    each(1, N, lambda r: g2_copy(r).start())
    g2r[my] = g2s[...]

    c2_core.wait_recv()

    def first_arrives(s):
        @pl.when(jnp.logical_not(jnp.logical_and(my == mx, 2 * s + half == my)))
        def _():
            send(fms.at[0], fmr.at[s], p2s.at[0], p2r.at[s], other).wait_recv()

    each(0, 8, first_arrives)
    for s in range(8):
        part = fmr[s].astype(F32)
        for t in range(4):
            lhsf[BLK * t : BLK * t + BLK, 32 * s : 32 * s + 32] = part[:, 32 * t : 32 * t + 32]
    lhs = lhsf[...].astype(BF16)
    low_lanes = lax.broadcasted_iota(jnp.int32, (BLK, 128), 1) < BLK
    for u in range(4):
        rhs = c2all[:, :, :, 256 * u : 256 * u + 256].reshape(256, 256)
        got = jnp.dot(lhs, rhs, preferred_element_type=F32)
        for v in range(2):
            for p in range(2):
                first = got[2 * BLK * p : 2 * BLK * p + BLK, 128 * v : 128 * v + 128]
                second = got[2 * BLK * p + BLK : 2 * BLK * p + 2 * BLK, 128 * v : 128 * v + 128]
                g = 4 * u + 2 * v
                sms[g, p] = jnp.where(low_lanes, first, pltpu.roll(second, BLK, 1)).astype(BF16)
                sms[g + 1, p] = jnp.where(low_lanes, pltpu.roll(first, BLK, 1), second).astype(BF16)

    def p3_copy(r):
        return send(
            sms.at[gy_peer(r)], rr.at[pl.ds(2 * my, 2)], p3s.at[r], p3r.at[r], (mx, gy_peer(r))
        )

    each(1, N, lambda r: p3_copy(r).start())
    rr[pl.ds(2 * my, 2)] = sms[my]

    each(1, N, lambda r: g2_copy(r).wait_recv())
    g3s[...] = jnp.sum(g2r[...], axis=0)
    g3s[4:5] = g2s[4:5]
    each(1, N, lambda r: g3_copy(r).start())
    g3r[mx] = g3s[...]

    each(1, N, lambda r: m1_copy(r).wait_recv())
    m1_out[...] = jnp.sum(m1r[...], axis=0)
    each(1, N, lambda r: g3_copy(r).wait_recv())
    m23_out[...] = g3r[...]
    each(1, N, lambda r: p3_copy(r).wait_recv())
    rr_out[...] = rr[...]

    for step in range(1, 5):
        z_copy(1, step).wait_send()
    for step in range(1, 4):
        z_copy(-1, step).wait_send()
    for o in OFFSETS:
        y_copy(o, 0).wait_send()
        y_copy(o, 1).wait_send()
    c2_y.wait_send()
    each(1, 4, lambda r: c2_x(r).wait_send())
    c2_core.wait_send()
    f_forward(0).wait_send()

    def left(r):
        f_copy(r).wait_send()
        f_forward(r).wait_send()
        g1_copy(r).wait_send()
        m1_copy(r).wait_send()
        g2_copy(r).wait_send()
        g3_copy(r).wait_send()
        p3_copy(r).wait_send()

    each(1, N, left)
    for m in range(8):

        @pl.when(not_self(m))
        def _():
            m_copy(m).wait_send()


CHUNK = 10


def hours_kernel(rr_ref, c3_ref, m1_ref, m23_ref, core_out, one_out, two_out, three_out, rrf, c3b, lhs):
    step = pl.program_id(0)

    @pl.when(step == 0)
    def _():
        for r in range(32):
            rrf[BLK * r : BLK * r + BLK, :] = rr_ref[r].astype(F32)
        row = lax.broadcasted_iota(jnp.int32, (64, 64), 0)
        hour = lax.broadcasted_iota(jnp.int32, (64, 64), 1)
        evens_first = hour == jnp.where(row < 32, 2 * row, 2 * row - 63)
        c3b[...] = jnp.dot(
            evens_first.astype(BF16), c3_ref[...], preferred_element_type=F32
        ).astype(BF16)
        one_out[...] = m1_ref[0:6, :]
        for g in range(N):
            three_out[4 * g : 4 * g + 4, :] = m23_ref[g, 0:4]
            two_out[g : g + 1, :] = m23_ref[g, 4:5]

    for k in range(CHUNK):
        turned = rrf[pl.ds(step * CHUNK + k, 32, stride=BLK), :].T
        lhs[56 * k : 56 * k + 56, 0:32] = turned[0:56]
        lhs[56 * k : 56 * k + 56, 32:64] = turned[BLK : BLK + 56]
    got = jnp.dot(lhs[...].astype(BF16), c3b[...], preferred_element_type=F32)
    for k in range(CHUNK):
        core_out[k] = got[56 * k : 56 * k + 50]


def on_device(
    field_slab, one_by_second, one_by_hours, two_by_first, two_by_hours,
    three_by_first, three_by_second, core_first, core_second, core_hours,
):
    vmem = pl.BlockSpec(memory_space=pltpu.VMEM)
    dma = pltpu.SemaphoreType.DMA
    rr, m1, m23 = pl.pallas_call(
        exchange_kernel,
        out_shape=(
            jax.ShapeDtypeStruct((32, BLK, 128), BF16),
            jax.ShapeDtypeStruct((8, 400), F32),
            jax.ShapeDtypeStruct((N, 8, 400), F32),
        ),
        in_specs=[vmem] * 9,
        out_specs=(vmem, vmem, vmem),
        scratch_shapes=[
            pltpu.VMEM((1024, 128), F32),
            pltpu.VMEM((N, 4, 16, 96), BF16),
            pltpu.VMEM((N, 4, 2, 16, 96), BF16),
            pltpu.VMEM((N, 96, WIN), BF16),
            pltpu.VMEM((16, 1024), F32),
            pltpu.VMEM((8, 2, 16, 1024), BF16),
            pltpu.VMEM((16, 400), F32),
            pltpu.VMEM((16, 400), F32),
            pltpu.VMEM((128, WIN), F32),
            pltpu.VMEM((WIN, 128), F32),
            pltpu.VMEM((8, BLK, 128), BF16),
            pltpu.VMEM((8, BLK, 128), BF16),
            pltpu.VMEM((256, 256), F32),
            pltpu.VMEM((N, 2, BLK, 128), BF16),
            pltpu.VMEM((32, BLK, 128), BF16),
            pltpu.VMEM((96, 400), F32),
            pltpu.VMEM((16, 400), F32),
            pltpu.VMEM((64, 400), F32),
            pltpu.VMEM((N, 8, 400), F32),
            pltpu.VMEM((N, 8, 400), F32),
            pltpu.VMEM((N, 8, 400), F32),
            pltpu.VMEM((N, 8, 400), F32),
            pltpu.VMEM((8, 400), F32),
            pltpu.VMEM((N, 8, 400), F32),
            pltpu.VMEM((8, 400), F32),
            pltpu.VMEM((N, 8, 400), F32),
            dma((N,)), dma((N,)), dma((N,)), dma((N,)),
            dma((7,)), dma((7,)), dma((16,)), dma((16,)),
            dma((5,)), dma((5,)), dma((8,)), dma((8,)), dma((N,)), dma((N,)),
            dma((N,)), dma((N,)), dma((N,)), dma((N,)), dma((N,)), dma((N,)), dma((N,)), dma((N,)),
        ],
        compiler_params=pltpu.CompilerParams(
            collective_id=0, has_side_effects=True, vmem_limit_bytes=32 * 2**20
        ),
        cost_estimate=pl.CostEstimate(flops=500_000_000, bytes_accessed=2_000_000, transcendentals=0),
        name="exchange",
    )(
        jnp.transpose(field_slab, (1, 2, 0)), core_first.T, core_second.T,
        one_by_second, one_by_hours, two_by_first, two_by_hours, three_by_first, three_by_second,
    )

    def whole(shape):
        return pl.BlockSpec(shape, lambda step: (0,) * len(shape))

    core_sketch, mode_one, mode_two, mode_three = pl.pallas_call(
        hours_kernel,
        grid=(50 // CHUNK,),
        out_shape=(
            jax.ShapeDtypeStruct((50, 50, 800), F32),
            jax.ShapeDtypeStruct((6, 400), F32),
            jax.ShapeDtypeStruct((16, 400), F32),
            jax.ShapeDtypeStruct((64, 400), F32),
        ),
        in_specs=[whole((32, BLK, 128)), whole((64, 800)), whole((8, 400)), whole((N, 8, 400))],
        out_specs=(
            pl.BlockSpec((CHUNK, 50, 800), lambda step: (step, 0, 0)),
            whole((6, 400)), whole((16, 400)), whole((64, 400)),
        ),
        scratch_shapes=[
            pltpu.VMEM((32 * BLK, 128), F32),
            pltpu.VMEM((64, 800), BF16),
            pltpu.VMEM((56 * CHUNK, 64), F32),
        ],
        compiler_params=pltpu.CompilerParams(vmem_limit_bytes=32 * 2**20),
        cost_estimate=pl.CostEstimate(flops=260_000_000, bytes_accessed=11_000_000, transcendentals=0),
        name="hours",
    )(rr, core_hours.T, m1, m23)
    return mode_one, mode_two, mode_three, core_sketch


def solution(mesh):
    in_specs = (
        P("gx", "gy", None),
        P("gy", None),
        P(),
        P("gx", None),
        P(),
        P("gx", None),
        P("gy", None),
        P(None, "gx"),
        P(None, "gy"),
        P(),
    )
    out_specs = (P(("gx", "gy"), None), P("gy", None), P(), P("gx", "gy", None))
    return jax.shard_map(
        on_device, mesh=mesh, in_specs=in_specs, out_specs=out_specs, check_vma=False
    )
```

```python
import jax
import jax.numpy as jnp
from jax import lax
from jax.experimental import pallas as pl
from jax.experimental.pallas import tpu as pltpu
from jax.sharding import PartitionSpec as P

MESH = pl.DeviceIdType.MESH
F32 = jnp.float32
BF16 = jnp.bfloat16
N = 16
NZ = 8
WIN = 256
BLK = 64
OFFSETS = (0, -1, 1, -2, 2, -3, 3, -4)


def exchange_kernel(
    f_hbm, cf_hbm, c2_hbm, c3_hbm, s1_hbm, h1_hbm, f2_hbm, h2_hbm, f3_hbm, s3_hbm,
    rr_out, c3_out, one_out, two_out, three_out,
    f_ref, cf_ref, c2_ref, c3_ref, s1_ref, h1_ref, f2_ref, h2_ref, f3_ref, s3_ref,
    f32s, fblk, fall, cfall, c2f, c2all, s1f, s3f, acc, acct, fms, fmr, lhsf, sms, rr,
    m1a, m2a, m3a, a1s, a1r, t2s, t2r, g2s, g2r, g3s, g3r,
    loads, fs, fr, fxs, fxr, fcs, fcr, zs, zr, ys, yr, cs, cr, p2s, p2r, p3s, p3r,
    a1ss, a1rs, t2ss, t2rs, g2ss, g2rs, g3ss, g3rs,
):
    mx, my = lax.axis_index("gx"), lax.axis_index("gy")
    ylo, z = lax.rem(mx, 2), mx // 2
    core, yhi, x = lax.rem(my, 2), lax.rem(my // 2, 2), my // 4
    xlo, xhi = lax.rem(x, 2), x // 2
    quarter, four = 2 * xlo + core, 2 * xhi + yhi
    other_core = (mx, my + 1 - 2 * core)
    other_x = (mx, my + 4 - 8 * xlo)
    y = 2 * yhi + ylo

    def at_y(there):
        there = lax.rem(there, 4)
        return (2 * z + lax.rem(there, 2), 4 * x + 2 * (there // 2) + core)

    y_up, y_down = at_y(y + 1), at_y(y + 3)
    z_up = (2 * lax.rem(z + 1, NZ) + ylo, my)
    z_down = (2 * lax.rem(z + NZ - 1, NZ) + ylo, my)

    def send(src, dst, send_sem, recv_sem, device):
        return pltpu.make_async_remote_copy(
            src_ref=src, dst_ref=dst, send_sem=send_sem, recv_sem=recv_sem,
            device_id=device, device_id_type=MESH,
        )

    def gx_peer(r):
        return lax.rem(mx + r, N)

    def gy_peer(r):
        return lax.rem(my + r, N)

    def each(low, high, body):
        def step(i, carry):
            body(i)
            return carry

        lax.fori_loop(low, high, step, 0)

    pairs = (
        (f_hbm, f_ref), (cf_hbm, cf_ref), (c2_hbm, c2_ref), (h1_hbm, h1_ref), (h2_hbm, h2_ref),
        (f2_hbm, f2_ref), (f3_hbm, f3_ref), (s1_hbm, s1_ref), (s3_hbm, s3_ref), (c3_hbm, c3_ref),
    )
    load = [pltpu.make_async_copy(src, dst, loads.at[i]) for i, (src, dst) in enumerate(pairs)]
    for one in load:
        one.start()

    barrier = pltpu.get_barrier_semaphore()

    def greet(r):
        pl.semaphore_signal(barrier, inc=1, device_id=(gx_peer(r), my), device_id_type=MESH)
        pl.semaphore_signal(barrier, inc=1, device_id=(mx, gy_peer(r)), device_id_type=MESH)

    each(1, N, greet)
    across = (mx + 1 - 2 * ylo, my + 2 - 4 * yhi)
    pl.semaphore_signal(barrier, inc=1, device_id=across, device_id_type=MESH)

    load[1].wait()
    cfall[mx, :, 128:256] = jnp.zeros((96, 128), BF16)
    for q in range(4):

        @pl.when(quarter == q)
        def _():
            cfall[mx, :, 0:200] = cf_ref[:, 200 * q : 200 * q + 200]

    load[0].wait()
    for j in range(16):
        f32s[64 * j : 64 * j + 64, 0:96] = f_ref[j].astype(F32)
    for t in range(64):
        fblk[t // 4, t % 4] = f32s[pl.ds(t, 16, stride=64), :][:, 0:96].astype(BF16)
    for t in range(4):
        fall[mx, t, quarter] = fblk[mx, t]

    pl.semaphore_wait(barrier, 2 * (N - 1) + 1)

    def shard(o, low):
        return 2 * lax.rem(z + o + NZ, NZ) + low

    def z_copy(direction, step):
        o = -direction * (step - 1)
        index = step - 1 if direction > 0 else 3 + step
        slot = cfall.at[shard(o, ylo)]
        return send(slot, slot, zs.at[index], zr.at[index], z_up if direction > 0 else z_down)

    def y_copy(o, h):
        slot = cfall.at[shard(o, ylo), pl.ds(48 * h, 48)]
        index = 2 * (o + 4) + h
        return send(slot, slot, ys.at[index], yr.at[index], y_up if h == 0 else y_down)

    def pass_on(o):
        y_copy(o, 0).start()
        y_copy(o, 1).start()

    def ring(step):
        z_copy(1, step).wait_recv()
        if step < 4:
            z_copy(1, step + 1).start()
            z_copy(-1, step).wait_recv()
            if step < 3:
                z_copy(-1, step + 1).start()
        pass_on(-step)
        if step < 4:
            pass_on(step)

    def f_copy(r):
        return send(
            fblk.at[gx_peer(r)], fall.at[mx, :, quarter], fs.at[r], fr.at[r], (gx_peer(r), my)
        )

    def f_x(r):
        slot = fall.at[lax.rem(mx + N - r, N), :, quarter]
        return send(slot, slot, fxs.at[r], fxr.at[r], other_x)

    own_columns = fall.at[:, :, quarter]
    f_core = send(own_columns, own_columns, fcs.at[0], fcr.at[0], other_core)
    x_columns = fall.at[:, :, quarter + 2 - 4 * xlo]
    f_x_core = send(x_columns, x_columns, fcs.at[1], fcr.at[1], other_core)

    z_copy(1, 1).start()
    z_copy(-1, 1).start()
    pass_on(0)
    each(1, N, lambda r: f_copy(r).start())
    f_x(0).start()

    for one in load[2:]:
        one.wait()
    s1f[...] = s1_ref[...].astype(F32)
    s3f[...] = s3_ref[...].astype(F32)
    m1a[...] = jnp.zeros_like(m1a)
    m3a[...] = jnp.zeros_like(m3a)

    def modes(low, high):
        def one(j):
            rows = f_ref[j]
            turned = (((0,), (0,)), ((), ()))
            by_one = lax.dot_general(rows, h1_ref[...], turned, preferred_element_type=F32)
            m1a[...] += by_one * s1f[pl.ds(j, 1), :]
            by_two = lax.dot_general(rows, h2_ref[...], turned, preferred_element_type=F32)
            m2a[pl.ds(j, 1), :] = jnp.sum(by_two * f2_ref[...].astype(F32), axis=0, keepdims=True)
            by_three = jnp.dot(rows, f3_ref[...], preferred_element_type=F32)
            m3a[...] += by_three * s3f[pl.ds(j, 1), :]

        each(low, high, one)

    modes(0, 8)
    ring(1)
    modes(8, 16)

    def a1_copy(r):
        return send(a1s.at[gy_peer(r)], a1r.at[my], a1ss.at[r], a1rs.at[r], (mx, gy_peer(r)))

    def t2_copy(r):
        return send(t2s.at[gx_peer(r)], t2r.at[mx], t2ss.at[r], t2rs.at[r], (gx_peer(r), my))

    def g2_copy(r):
        return send(g2s, g2r.at[mx], g2ss.at[r], g2rs.at[r], (gx_peer(r), my))

    def g3_copy(r):
        return send(g3s, g3r.at[my], g3ss.at[r], g3rs.at[r], (mx, gy_peer(r)))

    a1s[:, 1] = jnp.zeros((N, 4, 400), F32)
    for g in range(N):
        a1s[g, 0] = m1a[6 * g : 6 * g + 4]
        a1s[g, 1, 0:2] = m1a[6 * g + 4 : 6 * g + 6]
        a1s[g, 2] = m3a[4 * g : 4 * g + 4]
        t2s[g] = m2a[g : g + 1]

    def first_exchange(r):
        t2_copy(r).start()
        a1_copy(r).start()

    each(1, N, first_exchange)
    a1r[my] = a1s[my]
    t2r[mx] = t2s[mx]
    ring(2)

    c2f[...] = jnp.zeros_like(c2f)
    for g in range(N):
        c2f[:, BLK * g : BLK * g + 50] = c2_ref[:, 50 * g : 50 * g + 50].astype(F32)
    c2all[four, xlo, core] = c2f[...].astype(BF16)
    c2_own = c2all.at[four, xlo, core]
    c2_y = send(c2_own, c2_own, cs.at[0], cr.at[0], (mx, my + 2 - 4 * yhi))
    c2_y.start()

    def c2_x(r):
        pair = c2all.at[pl.ds(2 * xhi, 2), xlo, core]
        return send(
            pair, pair, cs.at[r], cr.at[r], (mx, 4 * lax.rem(x + r, 4) + 2 * yhi + core)
        )

    c2_mine = c2all.at[:, :, core]
    c2_core = send(c2_mine, c2_mine, cs.at[4], cr.at[4], other_core)

    def field_arrives(r):
        f_copy(r).wait_recv()
        f_x(r).start()

    each(1, N, field_arrives)
    f_core.start()
    ring(3)
    c2_y.wait_recv()
    each(1, 4, lambda r: c2_x(r).start())

    row = lax.broadcasted_iota(jnp.int32, (64, 64), 0)
    hour = lax.broadcasted_iota(jnp.int32, (64, 64), 1)
    evens_first = hour == jnp.where(row < 32, 2 * row, 2 * row - 63)
    c3_out[...] = jnp.dot(
        evens_first.astype(BF16), c3_ref[...], preferred_element_type=F32
    ).astype(BF16)
    ring(4)

    each(1, N, lambda r: a1_copy(r).wait_recv())
    each(1, N, lambda r: t2_copy(r).wait_recv())
    three = jnp.sum(a1r[:, 2], axis=0)
    for k in range(4):
        g2s[k] = three[k : k + 1]
    g2s[4] = jnp.sum(t2r[...], axis=0)
    each(1, N, lambda r: g2_copy(r).start())
    g2r[mx] = g2s[...]

    each(0, N, lambda r: f_x(r).wait_recv())
    f_x_core.start()
    one_out[0:4] = jnp.sum(a1r[:, 0], axis=0)
    one_out[4:8] = jnp.sum(a1r[:, 1], axis=0)
    each(1, 4, lambda r: c2_x(r).wait_recv())
    c2_core.start()

    def add_shard(g):
        acc[...] += jnp.dot(fall[g].reshape(256, 96), cfall[g], preferred_element_type=F32)

    acc[...] = jnp.zeros_like(acc)
    f_core.wait_recv()
    f_x_core.wait_recv()
    for o in OFFSETS:
        add_shard(shard(o, ylo))
        y_copy(o, 0).wait_recv()
        y_copy(o, 1).wait_recv()
        add_shard(shard(o, 1 - ylo))
    acct[...] = acc[...].T

    def m_copy(m):
        return send(fms.at[m], fmr.at[four], p2s.at[m], p2r.at[four], (4 * quarter + m, mx))

    def stays(m):
        return jnp.logical_and(4 * quarter + m == mx, mx == my)

    for m in range(4):
        fms[m] = acct[50 * m : 50 * m + BLK, :].astype(BF16)

        @pl.when(jnp.logical_not(stays(m)))
        def _():
            m_copy(m).start()

        @pl.when(stays(m))
        def _():
            fmr[four] = fms[m]

    each(1, N, lambda r: g2_copy(r).wait_recv())
    g3s[...] = jnp.concatenate([jnp.sum(g2r[:, k], axis=0) for k in range(4)], axis=0)
    each(1, N, lambda r: g3_copy(r).start())
    g3r[my] = g3s[...]
    for g in range(N):
        two_out[g : g + 1] = g2r[g, 4]
    c2_core.wait_recv()

    sent_quarter = mx // 4
    from_self = jnp.logical_and(mx == my, sent_quarter == quarter)

    def first_arrives(s):
        @pl.when(jnp.logical_not(jnp.logical_and(from_self, s == four)))
        def _():
            send(fms.at[0], fmr.at[s], p2s.at[0], p2r.at[s], other_core).wait_recv()

    each(0, 4, first_arrives)
    for s in range(4):
        part = fmr[s].astype(F32)
        for t in range(4):
            lhsf[BLK * t : BLK * t + BLK, BLK * s : BLK * s + BLK] = part[:, BLK * t : BLK * t + BLK]
    lhs = lhsf[...].astype(BF16)
    low_lanes = lax.broadcasted_iota(jnp.int32, (BLK, 128), 1) < BLK
    for u in range(4):
        rhs = c2all[:, :, :, :, 256 * u : 256 * u + 256].reshape(256, 256)
        got = jnp.dot(lhs, rhs, preferred_element_type=F32)
        for v in range(2):
            for p in range(2):
                first = got[2 * BLK * p : 2 * BLK * p + BLK, 128 * v : 128 * v + 128]
                second = got[2 * BLK * p + BLK : 2 * BLK * p + 2 * BLK, 128 * v : 128 * v + 128]
                g = 4 * u + 2 * v
                sms[g, p] = jnp.where(low_lanes, first, pltpu.roll(second, BLK, 1)).astype(BF16)
                sms[g + 1, p] = jnp.where(low_lanes, pltpu.roll(first, BLK, 1), second).astype(BF16)

    def p3_copy(r):
        return send(
            sms.at[gy_peer(r)], rr.at[pl.ds(2 * my, 2)], p3s.at[r], p3r.at[r], (mx, gy_peer(r))
        )

    each(1, N, lambda r: p3_copy(r).start())
    rr[pl.ds(2 * my, 2)] = sms[my]

    each(1, N, lambda r: g3_copy(r).wait_recv())
    for g in range(N):
        three_out[4 * g : 4 * g + 4] = g3r[g]

    for step in range(1, 5):
        z_copy(1, step).wait_send()
    for step in range(1, 4):
        z_copy(-1, step).wait_send()
    for o in OFFSETS:
        y_copy(o, 0).wait_send()
        y_copy(o, 1).wait_send()
    c2_y.wait_send()
    each(1, 4, lambda r: c2_x(r).wait_send())
    c2_core.wait_send()
    f_core.wait_send()
    f_x_core.wait_send()
    f_x(0).wait_send()

    def left(r):
        f_copy(r).wait_send()
        f_x(r).wait_send()
        a1_copy(r).wait_send()
        t2_copy(r).wait_send()
        g2_copy(r).wait_send()
        g3_copy(r).wait_send()

    each(1, N, left)
    for m in range(4):

        @pl.when(jnp.logical_not(stays(m)))
        def _():
            m_copy(m).wait_send()

    each(1, N, lambda r: p3_copy(r).wait_recv())
    rr_out[...] = rr[...]
    each(1, N, lambda r: p3_copy(r).wait_send())


CHUNK = 10


def hours_kernel(
    rr_ref, c3_ref, m1_ref, m2_ref, m3_ref, core_out, one_out, two_out, three_out, rrf, lhs
):
    step = pl.program_id(0)

    @pl.when(step == 0)
    def _():
        for r in range(32):
            rrf[BLK * r : BLK * r + BLK, :] = rr_ref[r].astype(F32)
        one_out[...] = m1_ref[0:6, :]
        two_out[...] = m2_ref[...]
        three_out[...] = m3_ref[...]

    for k in range(CHUNK):
        turned = rrf[pl.ds(step * CHUNK + k, 32, stride=BLK), :].T
        lhs[56 * k : 56 * k + 56, 0:32] = turned[0:56]
        lhs[56 * k : 56 * k + 56, 32:64] = turned[BLK : BLK + 56]
    got = jnp.dot(lhs[...].astype(BF16), c3_ref[...], preferred_element_type=F32)
    for k in range(CHUNK):
        core_out[k] = got[56 * k : 56 * k + 50]


def on_device(
    field_slab, one_by_second, one_by_hours, two_by_first, two_by_hours,
    three_by_first, three_by_second, core_first, core_second, core_hours,
):
    vmem = pl.BlockSpec(memory_space=pltpu.VMEM)
    hbm = pl.BlockSpec(memory_space=pltpu.HBM)
    dma = pltpu.SemaphoreType.DMA
    arguments = (
        jnp.transpose(field_slab, (1, 2, 0)), core_first.T, core_second.T, core_hours.T,
        one_by_second, one_by_hours, two_by_first, two_by_hours, three_by_first, three_by_second,
    )
    sizes = (
        ((32, BLK, 128), BF16), ((64, 800), BF16), ((8, 400), F32), ((16, 400), F32), ((64, 400), F32)
    )
    ways = [10, 16, 16, 16, 16, 2, 2, 7, 7, 16, 16, 5, 5, 4, 4, 16, 16] + [16] * 8
    between = pl.pallas_call(
        exchange_kernel,
        out_shape=tuple(jax.ShapeDtypeStruct(shape, dtype) for shape, dtype in sizes),
        in_specs=[hbm] * 10,
        out_specs=(vmem,) * 5,
        scratch_shapes=[pltpu.VMEM(a.shape, a.dtype) for a in arguments]
        + [
            pltpu.VMEM((1024, 128), F32),
            pltpu.VMEM((N, 4, 16, 96), BF16),
            pltpu.VMEM((N, 4, 4, 16, 96), BF16),
            pltpu.VMEM((N, 96, WIN), BF16),
            pltpu.VMEM((16, 1024), F32),
            pltpu.VMEM((4, 2, 2, 16, 1024), BF16),
            pltpu.VMEM((16, 400), F32),
            pltpu.VMEM((16, 400), F32),
            pltpu.VMEM((256, WIN), F32),
            pltpu.VMEM((WIN, 256), F32),
            pltpu.VMEM((4, BLK, 256), BF16),
            pltpu.VMEM((4, BLK, 256), BF16),
            pltpu.VMEM((256, 256), F32),
            pltpu.VMEM((N, 2, BLK, 128), BF16),
            pltpu.VMEM((32, BLK, 128), BF16),
            pltpu.VMEM((96, 400), F32),
            pltpu.VMEM((16, 400), F32),
            pltpu.VMEM((64, 400), F32),
            pltpu.VMEM((N, 3, 4, 400), F32),
            pltpu.VMEM((N, 3, 4, 400), F32),
            pltpu.VMEM((N, 1, 400), F32),
            pltpu.VMEM((N, 1, 400), F32),
            pltpu.VMEM((5, 1, 400), F32),
            pltpu.VMEM((N, 5, 1, 400), F32),
            pltpu.VMEM((4, 400), F32),
            pltpu.VMEM((N, 4, 400), F32),
        ]
        + [dma((n,)) for n in ways],
        compiler_params=pltpu.CompilerParams(
            collective_id=0, has_side_effects=True, vmem_limit_bytes=60 * 2**20
        ),
        cost_estimate=pl.CostEstimate(flops=500_000_000, bytes_accessed=2_000_000, transcendentals=0),
        name="exchange",
    )(*arguments)

    def whole(shape):
        return pl.BlockSpec(shape, lambda step: (0,) * len(shape))

    core_sketch, mode_one, mode_two, mode_three = pl.pallas_call(
        hours_kernel,
        grid=(50 // CHUNK,),
        out_shape=(
            jax.ShapeDtypeStruct((50, 50, 800), F32),
            jax.ShapeDtypeStruct((6, 400), F32),
            jax.ShapeDtypeStruct((16, 400), F32),
            jax.ShapeDtypeStruct((64, 400), F32),
        ),
        in_specs=[whole(shape) for shape, _ in sizes],
        out_specs=(
            pl.BlockSpec((CHUNK, 50, 800), lambda step: (step, 0, 0)),
            whole((6, 400)), whole((16, 400)), whole((64, 400)),
        ),
        scratch_shapes=[
            pltpu.VMEM((32 * BLK, 128), F32),
            pltpu.VMEM((56 * CHUNK, 64), F32),
        ],
        compiler_params=pltpu.CompilerParams(vmem_limit_bytes=60 * 2**20),
        cost_estimate=pl.CostEstimate(flops=260_000_000, bytes_accessed=11_000_000, transcendentals=0),
        name="hours",
    )(*between)
    return mode_one, mode_two, mode_three, core_sketch


def solution(mesh):
    in_specs = (
        P("gx", "gy", None),
        P("gy", None),
        P(),
        P("gx", None),
        P(),
        P("gx", None),
        P("gy", None),
        P(None, "gx"),
        P(None, "gy"),
        P(),
    )
    out_specs = (P(("gx", "gy"), None), P("gy", None), P(), P("gx", "gy", None))
    return jax.shard_map(
        on_device, mesh=mesh, in_specs=in_specs, out_specs=out_specs, check_vma=False
    )
```

```python
import jax
import jax.numpy as jnp
from jax import lax
from jax.experimental import pallas as pl
from jax.experimental.pallas import tpu as pltpu
from jax.sharding import PartitionSpec as P

MESH = pl.DeviceIdType.MESH
F32 = jnp.float32
BF16 = jnp.bfloat16
N = 16
NZ = 8
WIN = 256
ROWS = 112
BLK = 64
OFFSETS = (0, -1, 1, -2, 2, -3, 3, -4)


def exchange_kernel(
    f_hbm, cf_hbm, c2_hbm, c3_hbm, s1_hbm, h1_hbm, f2_hbm, h2_hbm, f3_hbm, s3_hbm,
    rr_out, c3_out, one_out, two_out, three_out,
    f_ref, cf_ref, c2_ref, c3_ref, s1_ref, h1_ref, f2_ref, h2_ref, f3_ref, s3_ref,
    f32s, fblk, fall, cfall, c2f, c2all, s1f, s3f, acct, fms, fmr, lhsf, sms, rr,
    c3v, onev, twov, threev, m1a, m2a, m3a, m1s, m1r, t3s, t3r, t2s, t2r, g2s, g2r, g3s, g3r,
    loads, stores, keeps, fs, fr, fxs, fxr, fxcs, fxcr, fcs, fcr, zs, zr, ys, yr, cs, cr, p2s, p2r, p3s, p3r,
    m1ss, m1rs, t3ss, t3rs, t2ss, t2rs, g2ss, g2rs, g3ss, g3rs,
):
    mx, my = lax.axis_index("gx"), lax.axis_index("gy")
    ylo, z = lax.rem(mx, 2), mx // 2
    core, yhi, x = lax.rem(my, 2), lax.rem(my // 2, 2), my // 4
    xlo, xhi = lax.rem(x, 2), x // 2
    quarter, four = 2 * xlo + core, 2 * xhi + yhi
    other_core = (mx, my + 1 - 2 * core)
    other_x = (mx, my + 4 - 8 * xlo)
    y = 2 * yhi + ylo

    def at_y(there):
        there = lax.rem(there, 4)
        return (2 * z + lax.rem(there, 2), 4 * x + 2 * (there // 2) + core)

    y_up, y_down = at_y(y + 1), at_y(y + 3)
    z_up = (2 * lax.rem(z + 1, NZ) + ylo, my)
    z_down = (2 * lax.rem(z + NZ - 1, NZ) + ylo, my)

    def send(src, dst, send_sem, recv_sem, device):
        return pltpu.make_async_remote_copy(
            src_ref=src, dst_ref=dst, send_sem=send_sem, recv_sem=recv_sem,
            device_id=device, device_id_type=MESH,
        )

    def gx_peer(r):
        return lax.rem(mx + r, N)

    def gy_peer(r):
        return lax.rem(my + r, N)

    def each(low, high, body):
        def step(i, carry):
            body(i)
            return carry

        lax.fori_loop(low, high, step, 0)

    pairs = (
        (f_hbm, f_ref), (cf_hbm, cf_ref), (c2_hbm, c2_ref), (h1_hbm, h1_ref), (h2_hbm, h2_ref),
        (f2_hbm, f2_ref), (f3_hbm, f3_ref), (s1_hbm, s1_ref), (s3_hbm, s3_ref), (c3_hbm, c3_ref),
    )
    load = [pltpu.make_async_copy(src, dst, loads.at[i]) for i, (src, dst) in enumerate(pairs)]
    for one in load:
        one.start()
    results = ((c3v, c3_out), (onev, one_out), (twov, two_out), (threev, three_out))
    store = [pltpu.make_async_copy(src, dst, stores.at[i]) for i, (src, dst) in enumerate(results)]

    barrier = pltpu.get_barrier_semaphore()

    def greet(r):
        pl.semaphore_signal(barrier, inc=1, device_id=(gx_peer(r), my), device_id_type=MESH)
        pl.semaphore_signal(barrier, inc=1, device_id=(mx, gy_peer(r)), device_id_type=MESH)

    each(1, N, greet)
    across = (mx + 1 - 2 * ylo, my + 2 - 4 * yhi)
    pl.semaphore_signal(barrier, inc=1, device_id=across, device_id_type=MESH)

    load[1].wait()
    cfall[mx, :, 128:256] = jnp.zeros((96, 128), BF16)
    for q in range(4):

        @pl.when(quarter == q)
        def _():
            cfall[mx, :, 0:200] = cf_ref[:, 200 * q : 200 * q + 200]

    load[0].wait()
    for j in range(16):
        f32s[64 * j : 64 * j + 64, 0:96] = f_ref[j].astype(F32)
    for g in range(N):
        last = f32s[pl.ds(4 * g + 3, 16, stride=64), :]
        for k in range(3):
            rows = f32s[pl.ds(4 * g + k, 16, stride=64), :]
            fblk[g, k] = jnp.concatenate(
                [rows[:, 0:96], last[:, 32 * k : 32 * k + 32]], axis=1
            ).astype(BF16)
    for k in range(3):
        fall[mx, k, quarter] = fblk[mx, k]

    pl.semaphore_wait(barrier, 2 * (N - 1) + 1)

    def shard(o, low):
        return 2 * lax.rem(z + o + NZ, NZ) + low

    def z_copy(direction, step):
        o = -direction * (step - 1)
        index = step - 1 if direction > 0 else 3 + step
        slot = cfall.at[shard(o, ylo)]
        return send(slot, slot, zs.at[index], zr.at[index], z_up if direction > 0 else z_down)

    def y_copy(o, h):
        slot = cfall.at[shard(o, ylo), pl.ds(48 * h, 48)]
        index = 2 * (o + 4) + h
        return send(slot, slot, ys.at[index], yr.at[index], y_up if h == 0 else y_down)

    def pass_on(o):
        y_copy(o, 0).start()
        y_copy(o, 1).start()

    def ring(step):
        z_copy(1, step).wait_recv()
        if step < 4:
            z_copy(1, step + 1).start()
            z_copy(-1, step).wait_recv()
            if step < 3:
                z_copy(-1, step + 1).start()
        pass_on(-step)
        if step < 4:
            pass_on(step)

    def f_copy(r):
        return send(
            fblk.at[gx_peer(r)], fall.at[mx, :, quarter], fs.at[r], fr.at[r], (gx_peer(r), my)
        )

    def f_x(r):
        slot = fall.at[lax.rem(mx + N - r, N), :, quarter]
        return send(slot, slot, fxs.at[r], fxr.at[r], other_x)

    own_columns = fall.at[:, :, quarter]
    f_core = send(own_columns, own_columns, fcs.at[0], fcr.at[0], other_core)

    def f_x_core(r):
        slot = fall.at[lax.rem(mx + N - r, N), :, quarter + 2 - 4 * xlo]
        return send(slot, slot, fxcs.at[r], fxcr.at[r], other_core)

    def x_arrives(r):
        f_x(r).wait_recv()
        f_x_core(r).start()


    c2_own = c2all.at[four, xlo, core]
    c2_y = send(c2_own, c2_own, cs.at[0], cr.at[0], (mx, my + 2 - 4 * yhi))

    def c2_x(r):
        pair = c2all.at[pl.ds(2 * xhi, 2), xlo, core]
        return send(
            pair, pair, cs.at[r], cr.at[r], (mx, 4 * lax.rem(x + r, 4) + 2 * yhi + core)
        )

    c2_mine = c2all.at[:, :, core]
    c2_core = send(c2_mine, c2_mine, cs.at[4], cr.at[4], other_core)

    z_copy(1, 1).start()
    z_copy(-1, 1).start()
    pass_on(0)
    each(1, N, lambda r: f_copy(r).start())
    f_x(0).start()

    for one in load[2:]:
        one.wait()
    s1f[...] = s1_ref[...].astype(F32)
    s3f[...] = s3_ref[...].astype(F32)
    m1a[...] = jnp.zeros_like(m1a)
    m3a[...] = jnp.zeros_like(m3a)

    def modes(low, high):
        def one(j):
            rows = f_ref[j]
            turned = (((0,), (0,)), ((), ()))
            by_one = lax.dot_general(rows, h1_ref[...], turned, preferred_element_type=F32)
            m1a[...] += by_one * s1f[pl.ds(j, 1), :]
            by_two = lax.dot_general(rows, h2_ref[...], turned, preferred_element_type=F32)
            m2a[pl.ds(j, 1), :] = jnp.sum(by_two * f2_ref[...].astype(F32), axis=0, keepdims=True)
            by_three = jnp.dot(rows, f3_ref[...], preferred_element_type=F32)
            m3a[...] += by_three * s3f[pl.ds(j, 1), :]

        each(low, high, one)

    modes(0, 8)
    ring(1)
    modes(8, 16)

    def m1_copy(r):
        return send(m1s.at[gy_peer(r)], m1r.at[my], m1ss.at[r], m1rs.at[r], (mx, gy_peer(r)))

    def t3_copy(r):
        return send(t3s.at[gy_peer(r)], t3r.at[my], t3ss.at[r], t3rs.at[r], (mx, gy_peer(r)))

    def t2_copy(r):
        return send(t2s.at[gx_peer(r)], t2r.at[mx], t2ss.at[r], t2rs.at[r], (gx_peer(r), my))

    def g2_copy(r):
        return send(g2s, g2r.at[mx], g2ss.at[r], g2rs.at[r], (gx_peer(r), my))

    def g3_copy(r):
        return send(g3s, g3r.at[my], g3ss.at[r], g3rs.at[r], (mx, gy_peer(r)))

    m1s[:, 1] = jnp.zeros((N, 4, 400), F32)
    for g in range(N):
        m1s[g, 0] = m1a[6 * g : 6 * g + 4]
        m1s[g, 1, 0:2] = m1a[6 * g + 4 : 6 * g + 6]
        t3s[g] = m3a[4 * g : 4 * g + 4]
        t2s[g] = m2a[g : g + 1]

    def first_exchange(r):
        t2_copy(r).start()
        t3_copy(r).start()

    each(1, N, first_exchange)
    t3r[my] = t3s[my]
    t2r[mx] = t2s[mx]
    ring(2)

    c2f[...] = jnp.zeros_like(c2f)
    for g in range(N):
        c2f[:, BLK * g : BLK * g + 50] = c2_ref[:, 50 * g : 50 * g + 50].astype(F32)
    c2all[four, xlo, core] = c2f[...].astype(BF16)
    c2_y.start()

    def field_arrives(r):
        f_copy(r).wait_recv()
        f_x(r).start()

    each(1, N, field_arrives)
    f_core.start()
    ring(3)
    c2_y.wait_recv()
    each(1, 4, lambda r: c2_x(r).start())

    row = lax.broadcasted_iota(jnp.int32, (64, 64), 0)
    hour = lax.broadcasted_iota(jnp.int32, (64, 64), 1)
    arranged = hour == 4 * (row & 15) + 2 * ((row >> 4) & 1) + (row >> 5)
    c3v[...] = jnp.dot(
        arranged.astype(BF16), c3_ref[...], preferred_element_type=F32
    ).astype(BF16)
    store[0].start()
    ring(4)

    each(1, N, lambda r: t3_copy(r).wait_recv())
    each(1, N, lambda r: t2_copy(r).wait_recv())
    three = jnp.sum(t3r[...], axis=0)
    for k in range(4):
        g2s[k] = three[k : k + 1]
    g2s[4] = jnp.sum(t2r[...], axis=0)
    each(1, N, lambda r: g2_copy(r).start())
    g2r[mx] = g2s[...]

    each(0, N, x_arrives)
    each(1, 4, lambda r: c2_x(r).wait_recv())
    c2_core.start()

    def total(side, wait):
        got = jnp.zeros((128, WIN), F32)
        for o in OFFSETS:
            for low in range(2):
                g = shard(o, (ylo + low) % 2)
                if low and wait:
                    y_copy(o, 0).wait_recv()
                    y_copy(o, 1).wait_recv()
                three = fall[g, :, pl.ds(2 * side, 2)].reshape(3, 32, 128)
                last = jnp.concatenate([three[k, :, 96:128] for k in range(3)], axis=1)
                rows = jnp.concatenate([three[k, :, 0:96] for k in range(3)] + [last], axis=0)
                got += jnp.dot(rows, cfall[g], preferred_element_type=F32)
        acct[side] = got.T

    f_core.wait_recv()
    total(xlo, True)
    each(0, N, lambda r: f_x_core(r).wait_recv())
    total(1 - xlo, False)

    def m_copy(m):
        return send(fms.at[m], fmr.at[four], p2s.at[m], p2r.at[four], (4 * quarter + m, mx))

    def stays(m):
        return jnp.logical_and(4 * quarter + m == mx, mx == my)

    for m in range(4):
        rows = slice(50 * m, 50 * m + BLK)
        fms[m] = jnp.concatenate([acct[0, rows], acct[1, rows]], axis=1).astype(BF16)

        @pl.when(jnp.logical_not(stays(m)))
        def _():
            m_copy(m).start()

        @pl.when(stays(m))
        def _():
            fmr[four] = fms[m]

    each(1, N, lambda r: m1_copy(r).start())
    m1r[my] = m1s[my]

    each(1, N, lambda r: g2_copy(r).wait_recv())
    g3s[...] = jnp.concatenate([jnp.sum(g2r[:, k], axis=0) for k in range(4)], axis=0)
    each(1, N, lambda r: g3_copy(r).start())
    g3r[my] = g3s[...]
    for g in range(N):
        twov[g : g + 1] = g2r[g, 4]
    store[2].start()
    c2_core.wait_recv()

    sent_quarter = mx // 4
    from_self = jnp.logical_and(mx == my, sent_quarter == quarter)

    def first_arrives(s):
        @pl.when(jnp.logical_not(jnp.logical_and(from_self, s == four)))
        def _():
            send(fms.at[0], fmr.at[s], p2s.at[0], p2r.at[s], other_core).wait_recv()

    each(0, 4, first_arrives)
    for s in range(4):
        part = fmr[s].astype(F32)
        for t in range(4):
            for side in range(2):
                to, at = BLK * s + 32 * side, 128 * side + 32 * t
                lhsf[BLK * t : BLK * t + BLK, to : to + 32] = part[:, at : at + 32]
    lhs = lhsf[...].astype(BF16)
    low_lanes = lax.broadcasted_iota(jnp.int32, (BLK, 128), 1) < BLK
    def p3_copy(g):
        return send(sms.at[g], rr.at[my], p3s.at[g], p3r.at[my], (mx, g))

    for ahead in (2, 1, 3, 0):
        u = lax.rem(x + ahead, 4)
        columns = pl.ds(pl.multiple_of(256 * u, 256), 256)
        rhs = c2all[:, :, :, :, columns].reshape(256, 256)
        got = jnp.dot(lhs, rhs, preferred_element_type=F32)
        for v in range(2):
            g = 4 * u + 2 * v
            lower, upper = [], []
            for p in range(2):
                tile = slice(128 * v, 128 * v + 128)
                first = got[2 * BLK * p : 2 * BLK * p + BLK, tile]
                second = got[2 * BLK * p + BLK : 2 * BLK * p + 2 * BLK, tile]
                lower.append(jnp.where(low_lanes, first, pltpu.roll(second, BLK, 1))[0:50])
                upper.append(jnp.where(low_lanes, pltpu.roll(first, BLK, 1), second)[0:50])
            fill = [jnp.zeros((ROWS - 100, 128), F32)]
            sms[g] = jnp.concatenate(lower + fill, axis=0).astype(BF16)
            sms[g + 1] = jnp.concatenate(upper + fill, axis=0).astype(BF16)
            for to in (g, g + 1):
                if ahead:
                    p3_copy(to).start()
                else:

                    @pl.when(to != my)
                    def _():
                        p3_copy(to).start()

    rr[my] = sms[my]

    each(1, N, lambda r: m1_copy(r).wait_recv())
    onev[0:4] = jnp.sum(m1r[:, 0], axis=0)
    onev[4:6] = jnp.sum(m1r[:, 1], axis=0)[0:2]
    store[1].start()
    each(1, N, lambda r: g3_copy(r).wait_recv())
    for g in range(N):
        threev[4 * g : 4 * g + 4] = g3r[g]
    store[3].start()

    for step in range(1, 5):
        z_copy(1, step).wait_send()
    for step in range(1, 4):
        z_copy(-1, step).wait_send()
    for o in OFFSETS:
        y_copy(o, 0).wait_send()
        y_copy(o, 1).wait_send()
    c2_y.wait_send()
    each(1, 4, lambda r: c2_x(r).wait_send())
    c2_core.wait_send()
    f_core.wait_send()
    f_x(0).wait_send()
    f_x_core(0).wait_send()

    def left(r):
        f_copy(r).wait_send()
        f_x(r).wait_send()
        f_x_core(r).wait_send()
        m1_copy(r).wait_send()
        t3_copy(r).wait_send()
        t2_copy(r).wait_send()
        g2_copy(r).wait_send()
        g3_copy(r).wait_send()

    each(1, N, left)
    for m in range(4):

        @pl.when(jnp.logical_not(stays(m)))
        def _():
            m_copy(m).wait_send()

    def second_arrives(r):
        send(sms.at[0], rr.at[0], p3s.at[0], p3r.at[gy_peer(r)], other_core).wait_recv()
        keep(gy_peer(r)).start()

    def keep(g):
        return pltpu.make_async_copy(rr.at[g], rr_out.at[g], keeps.at[g])

    keep(my).start()
    each(1, N, second_arrives)
    for one in store:
        one.wait()
    each(0, N, lambda g: keep(g).wait())
    each(1, N, lambda r: p3_copy(gy_peer(r)).wait_send())


CHUNKS = (3, 5, 8, 10, 12, 12)


def hours_kernel(
    rr_hbm, c3_hbm, m1_hbm, m2_hbm, m3_hbm, core_out, one_out, two_out, three_out,
    rr_ref, c3_ref, m1_ref, m2_ref, m3_ref, rrf, lhs, core_ref, loads, passes, stores,
):
    get_rr = pltpu.make_async_copy(rr_hbm, rr_ref, loads.at[0])
    get_c3 = pltpu.make_async_copy(c3_hbm, c3_ref, loads.at[1])
    get_rr.start()
    get_c3.start()
    modes = ((m1_hbm, m1_ref, one_out), (m2_hbm, m2_ref, two_out), (m3_hbm, m3_ref, three_out))
    taken = [pltpu.make_async_copy(a, b, passes.at[i]) for i, (a, b, _) in enumerate(modes)]
    passed = [pltpu.make_async_copy(b, c, passes.at[3 + i]) for i, (_, b, c) in enumerate(modes)]
    for one in taken:
        one.start()
    get_rr.wait()
    for g in range(N):
        rrf[ROWS * g : ROWS * g + ROWS, :] = rr_ref[g].astype(F32)
    get_c3.wait()
    for i in range(3):
        taken[i].wait()
        passed[i].start()

    stored, done = [], 0
    for i, chunk in enumerate(CHUNKS):
        for a in range(done, done + chunk):
            hours = [rrf[pl.ds(50 * p + a, N, stride=ROWS), :] for p in range(2)]
            turned = jnp.concatenate(hours, axis=0).T
            lhs[56 * a : 56 * a + 56, 0:32] = turned[0:56]
            lhs[56 * a : 56 * a + 56, 32:64] = turned[BLK : BLK + 56]
        got = jnp.dot(
            lhs[56 * done : 56 * (done + chunk)].astype(BF16), c3_ref[...],
            preferred_element_type=F32,
        )
        for k in range(chunk):
            core_ref[done + k] = got[56 * k : 56 * k + 50]
        rows = pl.ds(done, chunk)
        stored.append(pltpu.make_async_copy(core_ref.at[rows], core_out.at[rows], stores.at[i]))
        stored[-1].start()
        done += chunk
    for one in passed + stored:
        one.wait()


def on_device(
    field_slab, one_by_second, one_by_hours, two_by_first, two_by_hours,
    three_by_first, three_by_second, core_first, core_second, core_hours,
):
    hbm = pl.BlockSpec(memory_space=pltpu.HBM)
    dma = pltpu.SemaphoreType.DMA
    arguments = (
        jnp.transpose(field_slab, (1, 2, 0)), core_first.T, core_second.T, core_hours.T,
        one_by_second, one_by_hours, two_by_first, two_by_hours, three_by_first, three_by_second,
    )
    sizes = (
        ((N, ROWS, 128), BF16), ((64, 800), BF16), ((6, 400), F32), ((16, 400), F32), ((64, 400), F32)
    )
    ways = [10, 4, 16, 16, 16, 16, 16, 16, 16, 1, 1, 7, 7, 16, 16, 5, 5, 4, 4, 16, 16] + [16] * 10
    between = pl.pallas_call(
        exchange_kernel,
        out_shape=tuple(jax.ShapeDtypeStruct(shape, dtype) for shape, dtype in sizes),
        in_specs=[hbm] * 10,
        out_specs=(hbm,) * 5,
        scratch_shapes=[pltpu.VMEM(a.shape, a.dtype) for a in arguments]
        + [
            pltpu.VMEM((1024, 128), F32),
            pltpu.VMEM((N, 3, 16, 128), BF16),
            pltpu.VMEM((N, 3, 4, 16, 128), BF16),
            pltpu.VMEM((N, 96, WIN), BF16),
            pltpu.VMEM((16, 1024), F32),
            pltpu.VMEM((4, 2, 2, 16, 1024), BF16),
            pltpu.VMEM((16, 400), F32),
            pltpu.VMEM((16, 400), F32),
            pltpu.VMEM((2, WIN, 128), F32),
            pltpu.VMEM((4, BLK, 256), BF16),
            pltpu.VMEM((4, BLK, 256), BF16),
            pltpu.VMEM((256, 256), F32),
            pltpu.VMEM((N, ROWS, 128), BF16),
            pltpu.VMEM((N, ROWS, 128), BF16),
            pltpu.VMEM((64, 800), BF16),
            pltpu.VMEM((6, 400), F32),
            pltpu.VMEM((16, 400), F32),
            pltpu.VMEM((64, 400), F32),
            pltpu.VMEM((96, 400), F32),
            pltpu.VMEM((16, 400), F32),
            pltpu.VMEM((64, 400), F32),
            pltpu.VMEM((N, 2, 4, 400), F32),
            pltpu.VMEM((N, 2, 4, 400), F32),
            pltpu.VMEM((N, 4, 400), F32),
            pltpu.VMEM((N, 4, 400), F32),
            pltpu.VMEM((N, 1, 400), F32),
            pltpu.VMEM((N, 1, 400), F32),
            pltpu.VMEM((5, 1, 400), F32),
            pltpu.VMEM((N, 5, 1, 400), F32),
            pltpu.VMEM((4, 400), F32),
            pltpu.VMEM((N, 4, 400), F32),
        ]
        + [dma((n,)) for n in ways],
        compiler_params=pltpu.CompilerParams(
            collective_id=0, has_side_effects=True, vmem_limit_bytes=60 * 2**20
        ),
        cost_estimate=pl.CostEstimate(flops=500_000_000, bytes_accessed=2_000_000, transcendentals=0),
        name="exchange",
    )(*arguments)

    core_sketch, mode_one, mode_two, mode_three = pl.pallas_call(
        hours_kernel,
        out_shape=(
            jax.ShapeDtypeStruct((50, 50, 800), F32),
            jax.ShapeDtypeStruct((6, 400), F32),
            jax.ShapeDtypeStruct((16, 400), F32),
            jax.ShapeDtypeStruct((64, 400), F32),
        ),
        in_specs=[hbm] * 5,
        out_specs=(hbm,) * 4,
        scratch_shapes=[
            pltpu.VMEM((N, ROWS, 128), BF16),
            pltpu.VMEM((64, 800), BF16),
            pltpu.VMEM((6, 400), F32),
            pltpu.VMEM((16, 400), F32),
            pltpu.VMEM((64, 400), F32),
            pltpu.VMEM((N * ROWS, 128), F32),
            pltpu.VMEM((56 * 50, 64), F32),
            pltpu.VMEM((50, 50, 800), F32),
            dma((2,)), dma((6,)), dma((len(CHUNKS),)),
        ],
        compiler_params=pltpu.CompilerParams(vmem_limit_bytes=60 * 2**20),
        cost_estimate=pl.CostEstimate(flops=260_000_000, bytes_accessed=11_000_000, transcendentals=0),
        name="hours",
    )(*between)
    return mode_one, mode_two, mode_three, core_sketch


def solution(mesh):
    in_specs = (
        P("gx", "gy", None),
        P("gy", None),
        P(),
        P("gx", None),
        P(),
        P("gx", None),
        P("gy", None),
        P(None, "gx"),
        P(None, "gy"),
        P(),
    )
    out_specs = (P(("gx", "gy"), None), P("gy", None), P(), P("gx", "gy", None))
    return jax.shard_map(
        on_device, mesh=mesh, in_specs=in_specs, out_specs=out_specs, check_vma=False
    )
```

```python
import jax
import jax.numpy as jnp
from jax import lax
from jax.experimental import pallas as pl
from jax.experimental.pallas import tpu as pltpu
from jax.sharding import PartitionSpec as P

MESH = pl.DeviceIdType.MESH
F32 = jnp.float32
BF16 = jnp.bfloat16
N = 16
NZ = 8
WIN = 256
ROWS = 112
BLK = 64
OFFSETS = (0, -1, 1, -2, 2, -3, 3, -4)


def exchange_kernel(
    f_hbm, cf_hbm, c2_hbm, c3_hbm, s1_hbm, h1_hbm, f2_hbm, h2_hbm, f3_hbm, s3_hbm,
    rr_out, c3_out, one_out, two_out, three_out,
    f_ref, cf_ref, c2_ref, c3_ref, s1_ref, h1_ref, f2_ref, h2_ref, f3_ref, s3_ref,
    f32s, fblk, fall, cfall, c2f, c2all, s1f, s3f, acct, fms, fmr, lhsf, sms, rr,
    c3v, onev, twov, threev, m1a, m2a, m3a, m1s, m1r, t3s, t3r, t2s, t2r, g2s, g2r, g3s, g3r,
    loads, stores, keeps, fs, fr, fxs, fxr, fxcs, fxcr, fcs, fcr, zs, zr, ys, yr, cs, cr, p2s, p2r, p3s, p3r,
    m1ss, m1rs, t3ss, t3rs, t2ss, t2rs, g2ss, g2rs, g3ss, g3rs,
):
    mx, my = lax.axis_index("gx"), lax.axis_index("gy")
    ylo, z = lax.rem(mx, 2), mx // 2
    core, yhi, x = lax.rem(my, 2), lax.rem(my // 2, 2), my // 4
    xlo, xhi = lax.rem(x, 2), x // 2
    quarter, four = 2 * xlo + core, 2 * xhi + yhi
    other_core = (mx, my + 1 - 2 * core)
    other_x = (mx, my + 4 - 8 * xlo)
    y = 2 * yhi + ylo

    def at_y(there):
        there = lax.rem(there, 4)
        return (2 * z + lax.rem(there, 2), 4 * x + 2 * (there // 2) + core)

    y_up, y_down = at_y(y + 1), at_y(y + 3)
    z_up = (2 * lax.rem(z + 1, NZ) + ylo, my)
    z_down = (2 * lax.rem(z + NZ - 1, NZ) + ylo, my)

    def send(src, dst, send_sem, recv_sem, device):
        return pltpu.make_async_remote_copy(
            src_ref=src, dst_ref=dst, send_sem=send_sem, recv_sem=recv_sem,
            device_id=device, device_id_type=MESH,
        )

    def gx_peer(r):
        return lax.rem(mx + r, N)

    def gy_peer(r):
        return lax.rem(my + r, N)

    def each(low, high, body):
        for i in range(low, high):
            body(i)

    pairs = (
        (f_hbm, f_ref), (cf_hbm, cf_ref), (c2_hbm, c2_ref), (h1_hbm, h1_ref), (h2_hbm, h2_ref),
        (f2_hbm, f2_ref), (f3_hbm, f3_ref), (s1_hbm, s1_ref), (s3_hbm, s3_ref), (c3_hbm, c3_ref),
    )
    load = [pltpu.make_async_copy(src, dst, loads.at[i]) for i, (src, dst) in enumerate(pairs)]
    for one in load:
        one.start()
    results = ((c3v, c3_out), (onev, one_out), (twov, two_out), (threev, three_out))
    store = [pltpu.make_async_copy(src, dst, stores.at[i]) for i, (src, dst) in enumerate(results)]

    barrier = pltpu.get_barrier_semaphore()

    def greet(r):
        pl.semaphore_signal(barrier, inc=1, device_id=(gx_peer(r), my), device_id_type=MESH)
        pl.semaphore_signal(barrier, inc=1, device_id=(mx, gy_peer(r)), device_id_type=MESH)

    for r in (8, 9, 7, 10, 6, 11, 5, 12, 4, 13, 3, 14, 2, 15, 1):
        greet(r)
    across = (mx + 1 - 2 * ylo, my + 2 - 4 * yhi)
    pl.semaphore_signal(barrier, inc=1, device_id=across, device_id_type=MESH)

    load[1].wait()
    cfall[mx, :, 128:256] = jnp.zeros((96, 128), BF16)
    for q in range(4):

        @pl.when(quarter == q)
        def _():
            cfall[mx, :, 0:200] = cf_ref[:, 200 * q : 200 * q + 200]

    load[0].wait()
    for j in range(16):
        f32s[64 * j : 64 * j + 64, 0:96] = f_ref[j].astype(F32)
    for g in range(N):
        last = f32s[pl.ds(4 * g + 3, 16, stride=64), :]
        for k in range(3):
            rows = f32s[pl.ds(4 * g + k, 16, stride=64), :]
            fblk[g, k] = jnp.concatenate(
                [rows[:, 0:96], last[:, 32 * k : 32 * k + 32]], axis=1
            ).astype(BF16)
    fall[mx, quarter] = fblk[mx]

    pl.semaphore_wait(barrier, 2 * (N - 1) + 1)

    def shard(o, low):
        return 2 * lax.rem(z + o + NZ, NZ) + low

    def z_copy(direction, step):
        o = -direction * (step - 1)
        index = step - 1 if direction > 0 else 3 + step
        slot = cfall.at[shard(o, ylo)]
        return send(slot, slot, zs.at[index], zr.at[index], z_up if direction > 0 else z_down)

    def y_copy(o, h):
        slot = cfall.at[shard(o, ylo), pl.ds(48 * h, 48)]
        index = 2 * (o + 4) + h
        return send(slot, slot, ys.at[index], yr.at[index], y_up if h == 0 else y_down)

    def pass_on(o):
        y_copy(o, 0).start()
        y_copy(o, 1).start()

    def ring(step):
        z_copy(1, step).wait_recv()
        if step < 4:
            z_copy(1, step + 1).start()
            z_copy(-1, step).wait_recv()
            if step < 3:
                z_copy(-1, step + 1).start()
        pass_on(-step)
        if step < 4:
            pass_on(step)

    def f_copy(r):
        return send(
            fblk.at[gx_peer(r)], fall.at[mx, quarter], fs.at[r], fr.at[r], (gx_peer(r), my)
        )

    def f_x(r):
        slot = fall.at[lax.rem(mx + N - r, N), quarter]
        return send(slot, slot, fxs.at[r], fxr.at[r], other_x)

    own_columns = fall.at[:, quarter]
    f_core = send(own_columns, own_columns, fcs.at[0], fcr.at[0], other_core)

    def f_x_core(r):
        slot = fall.at[lax.rem(mx + N - r, N), quarter + 2 - 4 * xlo]
        return send(slot, slot, fxcs.at[r], fxcr.at[r], other_core)

    def x_arrives(r):
        f_x(r).wait_recv()
        f_x_core(r).start()


    c2_own = c2all.at[four, xlo, core]
    c2_y = send(c2_own, c2_own, cs.at[0], cr.at[0], (mx, my + 2 - 4 * yhi))

    def c2_x(r):
        pair = c2all.at[pl.ds(2 * xhi, 2), xlo, core]
        return send(
            pair, pair, cs.at[r], cr.at[r], (mx, 4 * lax.rem(x + r, 4) + 2 * yhi + core)
        )

    c2_mine = c2all.at[:, :, core]
    c2_core = send(c2_mine, c2_mine, cs.at[4], cr.at[4], other_core)

    z_copy(1, 1).start()
    z_copy(-1, 1).start()
    pass_on(0)
    each(1, N, lambda r: f_copy(r).start())
    f_x(0).start()

    for one in load[2:]:
        one.wait()
    s1f[...] = s1_ref[...].astype(F32)
    s3f[...] = s3_ref[...].astype(F32)
    m1a[...] = jnp.zeros_like(m1a)
    m3a[...] = jnp.zeros_like(m3a)

    def modes(low, high):
        def one(j):
            rows = f_ref[j]
            turned = (((0,), (0,)), ((), ()))
            by_one = lax.dot_general(rows, h1_ref[...], turned, preferred_element_type=F32)
            m1a[...] += by_one * s1f[pl.ds(j, 1), :]
            by_two = lax.dot_general(rows, h2_ref[...], turned, preferred_element_type=F32)
            m2a[pl.ds(j, 1), :] = jnp.sum(by_two * f2_ref[...].astype(F32), axis=0, keepdims=True)
            by_three = jnp.dot(rows, f3_ref[...], preferred_element_type=F32)
            m3a[...] += by_three * s3f[pl.ds(j, 1), :]

        each(low, high, one)

    modes(0, 8)
    ring(1)
    modes(8, 16)

    def m1_copy(r):
        return send(m1s.at[gy_peer(r)], m1r.at[my], m1ss.at[r], m1rs.at[r], (mx, gy_peer(r)))

    def t3_copy(r):
        return send(t3s.at[gy_peer(r)], t3r.at[my], t3ss.at[r], t3rs.at[r], (mx, gy_peer(r)))

    def t2_copy(r):
        return send(t2s.at[gx_peer(r)], t2r.at[mx], t2ss.at[r], t2rs.at[r], (gx_peer(r), my))

    def g2_copy(r):
        return send(g2s, g2r.at[mx], g2ss.at[r], g2rs.at[r], (gx_peer(r), my))

    def g3_copy(r):
        return send(g3s, g3r.at[my], g3ss.at[r], g3rs.at[r], (mx, gy_peer(r)))

    m1s[:, 1] = jnp.zeros((N, 4, 400), F32)
    for g in range(N):
        m1s[g, 0] = m1a[6 * g : 6 * g + 4]
        m1s[g, 1, 0:2] = m1a[6 * g + 4 : 6 * g + 6]
        t3s[g] = m3a[4 * g : 4 * g + 4]
        t2s[g] = m2a[g : g + 1]

    def first_exchange(r):
        t2_copy(r).start()
        t3_copy(r).start()

    each(1, N, first_exchange)
    t3r[my] = t3s[my]
    t2r[mx] = t2s[mx]
    ring(2)

    def field_arrives(r):
        f_copy(r).wait_recv()
        f_x(r).start()

    each(1, N, field_arrives)
    c2f[...] = jnp.zeros_like(c2f)
    for g in range(N):
        c2f[:, BLK * g : BLK * g + 50] = c2_ref[:, 50 * g : 50 * g + 50].astype(F32)
    c2all[four, xlo, core] = c2f[...].astype(BF16)
    c2_y.start()
    f_core.start()
    ring(3)
    c2_y.wait_recv()
    each(1, 4, lambda r: c2_x(r).start())

    row = lax.broadcasted_iota(jnp.int32, (64, 64), 0)
    hour = lax.broadcasted_iota(jnp.int32, (64, 64), 1)
    arranged = hour == 4 * (row & 15) + 2 * ((row >> 4) & 1) + (row >> 5)
    c3v[...] = jnp.dot(
        arranged.astype(BF16), c3_ref[...], preferred_element_type=F32
    ).astype(BF16)
    store[0].start()
    ring(4)

    each(1, N, lambda r: t3_copy(r).wait_recv())
    each(1, N, lambda r: t2_copy(r).wait_recv())
    three = jnp.sum(t3r[...], axis=0)
    for k in range(4):
        g2s[k] = three[k : k + 1]
    g2s[4] = jnp.sum(t2r[...], axis=0)
    each(1, N, lambda r: g2_copy(r).start())
    g2r[mx] = g2s[...]

    each(0, N, x_arrives)
    each(1, 4, lambda r: c2_x(r).wait_recv())
    c2_core.start()

    def total(side, wait):
        got = jnp.zeros((128, WIN), F32)
        for o in OFFSETS:
            for low in range(2):
                g = shard(o, (ylo + low) % 2)
                if low and wait:
                    y_copy(o, 0).wait_recv()
                    y_copy(o, 1).wait_recv()
                pair = fall[g, pl.ds(2 * side, 2)]
                three = [pair[:, k].reshape(32, 128) for k in range(3)]
                last = jnp.concatenate([three[k][:, 96:128] for k in range(3)], axis=1)
                rows = jnp.concatenate([three[k][:, 0:96] for k in range(3)] + [last], axis=0)
                got += jnp.dot(rows, cfall[g], preferred_element_type=F32)
        acct[side] = got.T

    f_core.wait_recv()
    total(xlo, True)
    each(0, N, lambda r: f_x_core(r).wait_recv())
    total(1 - xlo, False)

    def m_copy(m):
        return send(fms.at[m], fmr.at[four], p2s.at[m], p2r.at[four], (4 * quarter + m, mx))

    def stays(m):
        return jnp.logical_and(4 * quarter + m == mx, mx == my)

    for m in range(4):
        rows = slice(50 * m, 50 * m + BLK)
        fms[m] = jnp.concatenate([acct[0, rows], acct[1, rows]], axis=1).astype(BF16)

        @pl.when(jnp.logical_not(stays(m)))
        def _():
            m_copy(m).start()

        @pl.when(stays(m))
        def _():
            fmr[four] = fms[m]

    each(1, N, lambda r: m1_copy(r).start())
    m1r[my] = m1s[my]

    each(1, N, lambda r: g2_copy(r).wait_recv())
    g3s[...] = jnp.concatenate([jnp.sum(g2r[:, k], axis=0) for k in range(4)], axis=0)
    each(1, N, lambda r: g3_copy(r).start())
    g3r[my] = g3s[...]
    for g in range(N):
        twov[g : g + 1] = g2r[g, 4]
    store[2].start()
    c2_core.wait_recv()

    sent_quarter = mx // 4
    from_self = jnp.logical_and(mx == my, sent_quarter == quarter)

    def first_arrives(s):
        @pl.when(jnp.logical_not(jnp.logical_and(from_self, s == four)))
        def _():
            send(fms.at[0], fmr.at[s], p2s.at[0], p2r.at[s], other_core).wait_recv()

    each(0, 4, first_arrives)
    for s in range(4):
        part = fmr[s].astype(F32)
        for t in range(4):
            for side in range(2):
                to, at = BLK * s + 32 * side, 128 * side + 32 * t
                lhsf[BLK * t : BLK * t + BLK, to : to + 32] = part[:, at : at + 32]
    lhs = lhsf[...].astype(BF16)
    low_lanes = lax.broadcasted_iota(jnp.int32, (BLK, 128), 1) < BLK
    def p3_copy(g):
        return send(sms.at[g], rr.at[my], p3s.at[g], p3r.at[my], (mx, g))

    for ahead in (2, 1, 3, 0):
        u = lax.rem(x + ahead, 4)
        columns = pl.ds(pl.multiple_of(256 * u, 256), 256)
        rhs = c2all[:, :, :, :, columns].reshape(256, 256)
        got = jnp.dot(lhs, rhs, preferred_element_type=F32)
        for v in range(2):
            g = 4 * u + 2 * v
            lower, upper = [], []
            for p in range(2):
                tile = slice(128 * v, 128 * v + 128)
                first = got[2 * BLK * p : 2 * BLK * p + BLK, tile]
                second = got[2 * BLK * p + BLK : 2 * BLK * p + 2 * BLK, tile]
                lower.append(jnp.where(low_lanes, first, pltpu.roll(second, BLK, 1))[0:50])
                upper.append(jnp.where(low_lanes, pltpu.roll(first, BLK, 1), second)[0:50])
            fill = [jnp.zeros((ROWS - 100, 128), F32)]
            sms[g] = jnp.concatenate(lower + fill, axis=0).astype(BF16)
            sms[g + 1] = jnp.concatenate(upper + fill, axis=0).astype(BF16)
            for to in (g, g + 1):
                if ahead:
                    p3_copy(to).start()
                else:

                    @pl.when(to != my)
                    def _():
                        p3_copy(to).start()

    rr[my] = sms[my]

    each(1, N, lambda r: m1_copy(r).wait_recv())
    onev[0:4] = jnp.sum(m1r[:, 0], axis=0)
    onev[4:6] = jnp.sum(m1r[:, 1], axis=0)[0:2]
    store[1].start()
    each(1, N, lambda r: g3_copy(r).wait_recv())
    for g in range(N):
        threev[4 * g : 4 * g + 4] = g3r[g]
    store[3].start()

    for step in range(1, 5):
        z_copy(1, step).wait_send()
    for step in range(1, 4):
        z_copy(-1, step).wait_send()
    for o in OFFSETS:
        y_copy(o, 0).wait_send()
        y_copy(o, 1).wait_send()
    c2_y.wait_send()
    each(1, 4, lambda r: c2_x(r).wait_send())
    c2_core.wait_send()
    f_core.wait_send()
    f_x(0).wait_send()
    f_x_core(0).wait_send()

    def left(r):
        f_copy(r).wait_send()
        f_x(r).wait_send()
        f_x_core(r).wait_send()
        m1_copy(r).wait_send()
        t3_copy(r).wait_send()
        t2_copy(r).wait_send()
        g2_copy(r).wait_send()
        g3_copy(r).wait_send()

    each(1, N, left)
    for m in range(4):

        @pl.when(jnp.logical_not(stays(m)))
        def _():
            m_copy(m).wait_send()

    def second_arrives(r):
        send(sms.at[0], rr.at[0], p3s.at[0], p3r.at[gy_peer(r)], other_core).wait_recv()
        keep(gy_peer(r)).start()

    def keep(g):
        return pltpu.make_async_copy(rr.at[g], rr_out.at[g], keeps.at[g])

    keep(my).start()
    each(1, N, second_arrives)
    for one in store:
        one.wait()
    each(0, N, lambda g: keep(g).wait())
    each(1, N, lambda r: p3_copy(gy_peer(r)).wait_send())


CHUNKS = (3, 5, 8, 10, 12, 12)


def hours_kernel(
    rr_hbm, c3_hbm, m1_hbm, m2_hbm, m3_hbm, core_out, one_out, two_out, three_out,
    rr_ref, c3_ref, m1_ref, m2_ref, m3_ref, rrf, lhs, core_ref, loads, passes, stores,
):
    get_rr = pltpu.make_async_copy(rr_hbm, rr_ref, loads.at[0])
    get_c3 = pltpu.make_async_copy(c3_hbm, c3_ref, loads.at[1])
    get_rr.start()
    get_c3.start()
    modes = ((m1_hbm, m1_ref, one_out), (m2_hbm, m2_ref, two_out), (m3_hbm, m3_ref, three_out))
    taken = [pltpu.make_async_copy(a, b, passes.at[i]) for i, (a, b, _) in enumerate(modes)]
    passed = [pltpu.make_async_copy(b, c, passes.at[3 + i]) for i, (_, b, c) in enumerate(modes)]
    for one in taken:
        one.start()
    get_rr.wait()
    for g in range(N):
        rrf[ROWS * g : ROWS * g + ROWS, :] = rr_ref[g].astype(F32)
    get_c3.wait()
    for i in range(3):
        taken[i].wait()
        passed[i].start()

    stored, done = [], 0
    for i, chunk in enumerate(CHUNKS):
        for a in range(done, done + chunk):
            hours = [rrf[pl.ds(50 * p + a, N, stride=ROWS), :] for p in range(2)]
            turned = jnp.concatenate(hours, axis=0).T
            lhs[56 * a : 56 * a + 56, 0:32] = turned[0:56]
            lhs[56 * a : 56 * a + 56, 32:64] = turned[BLK : BLK + 56]
        got = jnp.dot(
            lhs[56 * done : 56 * (done + chunk)].astype(BF16), c3_ref[...],
            preferred_element_type=F32,
        )
        for k in range(chunk):
            core_ref[done + k] = got[56 * k : 56 * k + 50]
        rows = pl.ds(done, chunk)
        stored.append(pltpu.make_async_copy(core_ref.at[rows], core_out.at[rows], stores.at[i]))
        stored[-1].start()
        done += chunk
    for one in passed + stored:
        one.wait()


def on_device(
    field_slab, one_by_second, one_by_hours, two_by_first, two_by_hours,
    three_by_first, three_by_second, core_first, core_second, core_hours,
):
    hbm = pl.BlockSpec(memory_space=pltpu.HBM)
    dma = pltpu.SemaphoreType.DMA
    arguments = (
        jnp.transpose(field_slab, (1, 2, 0)), core_first.T, core_second.T, core_hours.T,
        one_by_second, one_by_hours, two_by_first, two_by_hours, three_by_first, three_by_second,
    )
    sizes = (
        ((N, ROWS, 128), BF16), ((64, 800), BF16), ((6, 400), F32), ((16, 400), F32), ((64, 400), F32)
    )
    ways = [10, 4, 16, 16, 16, 16, 16, 16, 16, 1, 1, 7, 7, 16, 16, 5, 5, 4, 4, 16, 16] + [16] * 10
    between = pl.pallas_call(
        exchange_kernel,
        out_shape=tuple(jax.ShapeDtypeStruct(shape, dtype) for shape, dtype in sizes),
        in_specs=[hbm] * 10,
        out_specs=(hbm,) * 5,
        scratch_shapes=[pltpu.VMEM(a.shape, a.dtype) for a in arguments]
        + [
            pltpu.VMEM((1024, 128), F32),
            pltpu.VMEM((N, 3, 16, 128), BF16),
            pltpu.VMEM((N, 4, 3, 16, 128), BF16),
            pltpu.VMEM((N, 96, WIN), BF16),
            pltpu.VMEM((16, 1024), F32),
            pltpu.VMEM((4, 2, 2, 16, 1024), BF16),
            pltpu.VMEM((16, 400), F32),
            pltpu.VMEM((16, 400), F32),
            pltpu.VMEM((2, WIN, 128), F32),
            pltpu.VMEM((4, BLK, 256), BF16),
            pltpu.VMEM((4, BLK, 256), BF16),
            pltpu.VMEM((256, 256), F32),
            pltpu.VMEM((N, ROWS, 128), BF16),
            pltpu.VMEM((N, ROWS, 128), BF16),
            pltpu.VMEM((64, 800), BF16),
            pltpu.VMEM((6, 400), F32),
            pltpu.VMEM((16, 400), F32),
            pltpu.VMEM((64, 400), F32),
            pltpu.VMEM((96, 400), F32),
            pltpu.VMEM((16, 400), F32),
            pltpu.VMEM((64, 400), F32),
            pltpu.VMEM((N, 2, 4, 400), F32),
            pltpu.VMEM((N, 2, 4, 400), F32),
            pltpu.VMEM((N, 4, 400), F32),
            pltpu.VMEM((N, 4, 400), F32),
            pltpu.VMEM((N, 1, 400), F32),
            pltpu.VMEM((N, 1, 400), F32),
            pltpu.VMEM((5, 1, 400), F32),
            pltpu.VMEM((N, 5, 1, 400), F32),
            pltpu.VMEM((4, 400), F32),
            pltpu.VMEM((N, 4, 400), F32),
        ]
        + [dma((n,)) for n in ways],
        compiler_params=pltpu.CompilerParams(
            collective_id=0, has_side_effects=True, vmem_limit_bytes=60 * 2**20
        ),
        cost_estimate=pl.CostEstimate(flops=500_000_000, bytes_accessed=2_000_000, transcendentals=0),
        name="exchange",
    )(*arguments)

    core_sketch, mode_one, mode_two, mode_three = pl.pallas_call(
        hours_kernel,
        out_shape=(
            jax.ShapeDtypeStruct((50, 50, 800), F32),
            jax.ShapeDtypeStruct((6, 400), F32),
            jax.ShapeDtypeStruct((16, 400), F32),
            jax.ShapeDtypeStruct((64, 400), F32),
        ),
        in_specs=[hbm] * 5,
        out_specs=(hbm,) * 4,
        scratch_shapes=[
            pltpu.VMEM((N, ROWS, 128), BF16),
            pltpu.VMEM((64, 800), BF16),
            pltpu.VMEM((6, 400), F32),
            pltpu.VMEM((16, 400), F32),
            pltpu.VMEM((64, 400), F32),
            pltpu.VMEM((N * ROWS, 128), F32),
            pltpu.VMEM((56 * 50, 64), F32),
            pltpu.VMEM((50, 50, 800), F32),
            dma((2,)), dma((6,)), dma((len(CHUNKS),)),
        ],
        compiler_params=pltpu.CompilerParams(vmem_limit_bytes=60 * 2**20),
        cost_estimate=pl.CostEstimate(flops=260_000_000, bytes_accessed=11_000_000, transcendentals=0),
        name="hours",
    )(*between)
    return mode_one, mode_two, mode_three, core_sketch


def solution(mesh):
    in_specs = (
        P("gx", "gy", None),
        P("gy", None),
        P(),
        P("gx", None),
        P(),
        P("gx", None),
        P("gy", None),
        P(None, "gx"),
        P(None, "gy"),
        P(),
    )
    out_specs = (P(("gx", "gy"), None), P("gy", None), P(), P("gx", "gy", None))
    return jax.shard_map(
        on_device, mesh=mesh, in_specs=in_specs, out_specs=out_specs, check_vma=False
    )
```

```python
import jax
import jax.numpy as jnp
from jax import lax
from jax.experimental import pallas as pl
from jax.experimental.pallas import tpu as pltpu
from jax.sharding import PartitionSpec as P

MESH = pl.DeviceIdType.MESH
F32 = jnp.float32
BF16 = jnp.bfloat16
N = 16
NZ = 8
WIN = 256
ROWS = 112
BLK = 64
OFFSETS = (0, -1, 1, -2, 2, -3, 3, -4)


def exchange_kernel(
    f_hbm, cf_hbm, c2_hbm, c3_hbm, s1_hbm, h1_hbm, f2_hbm, h2_hbm, f3_hbm, s3_hbm,
    rr_out, c3_out, one_out, two_out, three_out,
    f_ref, cf_ref, c2_ref, c3_ref, s1_ref, h1_ref, f2_ref, h2_ref, f3_ref, s3_ref,
    f32s, fblk, fall, cfall, c2f, c2all, s1f, s3f, acct, fms, fmr, lhsf, sms, rr,
    c3v, onev, twov, threev, m1a, m2a, m3a, m1s, m1r, t3s, t3r, t2s, t2r, g2s, g2r, g3s, g3r,
    loads, stores, keeps, fs, fr, fxs, fxr, fxcs, fxcr, fcs, fcr, zs, zr, ys, yr, cs, cr, p2s, p2r, p3s, p3r,
    m1ss, m1rs, t3ss, t3rs, t2ss, t2rs, g2ss, g2rs, g3ss, g3rs,
):
    mx, my = lax.axis_index("gx"), lax.axis_index("gy")
    ylo, z = lax.rem(mx, 2), mx // 2
    core, yhi, x = lax.rem(my, 2), lax.rem(my // 2, 2), my // 4
    xlo, xhi = lax.rem(x, 2), x // 2
    quarter, four = 2 * xlo + core, 2 * xhi + yhi
    other_core = (mx, my + 1 - 2 * core)
    other_x = (mx, my + 4 - 8 * xlo)
    y = 2 * yhi + ylo

    def at_y(there):
        there = lax.rem(there, 4)
        return (2 * z + lax.rem(there, 2), 4 * x + 2 * (there // 2) + core)

    y_up, y_down = at_y(y + 1), at_y(y + 3)
    z_up = (2 * lax.rem(z + 1, NZ) + ylo, my)
    z_down = (2 * lax.rem(z + NZ - 1, NZ) + ylo, my)

    def send(src, dst, send_sem, recv_sem, device):
        return pltpu.make_async_remote_copy(
            src_ref=src, dst_ref=dst, send_sem=send_sem, recv_sem=recv_sem,
            device_id=device, device_id_type=MESH,
        )

    def gx_peer(r):
        return lax.rem(mx + r, N)

    def gy_peer(r):
        return lax.rem(my + r, N)

    def each(low, high, body):
        for i in range(low, high):
            body(i)

    pairs = (
        (f_hbm, f_ref), (cf_hbm, cf_ref), (c2_hbm, c2_ref), (h1_hbm, h1_ref), (h2_hbm, h2_ref),
        (f2_hbm, f2_ref), (f3_hbm, f3_ref), (s1_hbm, s1_ref), (s3_hbm, s3_ref), (c3_hbm, c3_ref),
    )
    load = [pltpu.make_async_copy(src, dst, loads.at[i]) for i, (src, dst) in enumerate(pairs)]
    for one in load:
        one.start()
    results = ((c3v, c3_out), (onev, one_out), (twov, two_out), (threev, three_out))
    store = [pltpu.make_async_copy(src, dst, stores.at[i]) for i, (src, dst) in enumerate(results)]

    barrier = pltpu.get_barrier_semaphore()

    def greet(r):
        pl.semaphore_signal(barrier, inc=1, device_id=(gx_peer(r), my), device_id_type=MESH)
        pl.semaphore_signal(barrier, inc=1, device_id=(mx, gy_peer(r)), device_id_type=MESH)

    for r in (8, 9, 7, 10, 6, 11, 5, 12, 4, 13, 3, 14, 2, 15, 1):
        greet(r)
    across = (mx + 1 - 2 * ylo, my + 2 - 4 * yhi)
    pl.semaphore_signal(barrier, inc=1, device_id=across, device_id_type=MESH)

    load[1].wait()
    cfall[mx, :, 128:256] = jnp.zeros((96, 128), BF16)
    for q in range(4):

        @pl.when(quarter == q)
        def _():
            cfall[mx, :, 0:200] = cf_ref[:, 200 * q : 200 * q + 200]

    load[0].wait()
    for j in range(16):
        f32s[64 * j : 64 * j + 64, 0:96] = f_ref[j].astype(F32)
    for g in range(N):
        last = f32s[pl.ds(4 * g + 3, 16, stride=64), :]
        for k in range(3):
            rows = f32s[pl.ds(4 * g + k, 16, stride=64), :]
            fblk[g, k] = jnp.concatenate(
                [rows[:, 0:96], last[:, 32 * k : 32 * k + 32]], axis=1
            ).astype(BF16)
    fall[mx, quarter] = fblk[mx]

    pl.semaphore_wait(barrier, 2 * (N - 1) + 1)

    def shard(o, low):
        return 2 * lax.rem(z + o + NZ, NZ) + low

    def z_copy(direction, step):
        o = -direction * (step - 1)
        index = step - 1 if direction > 0 else 3 + step
        slot = cfall.at[shard(o, ylo)]
        return send(slot, slot, zs.at[index], zr.at[index], z_up if direction > 0 else z_down)

    def y_copy(o, h):
        slot = cfall.at[shard(o, ylo), pl.ds(48 * h, 48)]
        index = 2 * (o + 4) + h
        return send(slot, slot, ys.at[index], yr.at[index], y_up if h == 0 else y_down)

    def pass_on(o):
        y_copy(o, 0).start()
        y_copy(o, 1).start()

    def ring(step):
        z_copy(1, step).wait_recv()
        if step < 4:
            z_copy(1, step + 1).start()
            z_copy(-1, step).wait_recv()
            if step < 3:
                z_copy(-1, step + 1).start()
        pass_on(-step)
        if step < 4:
            pass_on(step)

    def f_copy(r):
        return send(
            fblk.at[gx_peer(r)], fall.at[mx, quarter], fs.at[r], fr.at[r], (gx_peer(r), my)
        )

    def f_x(r):
        slot = fall.at[lax.rem(mx + N - r, N), quarter]
        return send(slot, slot, fxs.at[r], fxr.at[r], other_x)

    own_columns = fall.at[:, quarter]
    f_core = send(own_columns, own_columns, fcs.at[0], fcr.at[0], other_core)

    def f_x_core(r):
        slot = fall.at[lax.rem(mx + N - r, N), quarter + 2 - 4 * xlo]
        return send(slot, slot, fxcs.at[r], fxcr.at[r], other_core)

    def x_arrives(r):
        f_x(r).wait_recv()
        f_x_core(r).start()


    c2_own = c2all.at[four, xlo, core]
    c2_y = send(c2_own, c2_own, cs.at[0], cr.at[0], (mx, my + 2 - 4 * yhi))

    def c2_x(r):
        pair = c2all.at[pl.ds(2 * xhi, 2), xlo, core]
        return send(
            pair, pair, cs.at[r], cr.at[r], (mx, 4 * lax.rem(x + r, 4) + 2 * yhi + core)
        )

    c2_mine = c2all.at[:, :, core]
    c2_core = send(c2_mine, c2_mine, cs.at[4], cr.at[4], other_core)

    z_copy(1, 1).start()
    z_copy(-1, 1).start()
    pass_on(0)
    each(1, N, lambda r: f_copy(r).start())
    f_x(0).start()

    for one in load[2:]:
        one.wait()
    s1f[...] = s1_ref[...].astype(F32)
    s3f[...] = s3_ref[...].astype(F32)
    m1a[...] = jnp.zeros_like(m1a)
    m3a[...] = jnp.zeros_like(m3a)

    def modes(low, high):
        def one(j):
            rows = f_ref[j]
            turned = (((0,), (0,)), ((), ()))
            by_one = lax.dot_general(rows, h1_ref[...], turned, preferred_element_type=F32)
            m1a[...] += by_one * s1f[pl.ds(j, 1), :]
            by_two = lax.dot_general(rows, h2_ref[...], turned, preferred_element_type=F32)
            m2a[pl.ds(j, 1), :] = jnp.sum(by_two * f2_ref[...].astype(F32), axis=0, keepdims=True)
            by_three = jnp.dot(rows, f3_ref[...], preferred_element_type=F32)
            m3a[...] += by_three * s3f[pl.ds(j, 1), :]

        each(low, high, one)

    modes(0, 8)
    ring(1)
    modes(8, 16)

    def m1_copy(r):
        return send(m1s.at[gy_peer(r)], m1r.at[my], m1ss.at[r], m1rs.at[r], (mx, gy_peer(r)))

    def t3_copy(r):
        return send(t3s.at[gy_peer(r)], t3r.at[my], t3ss.at[r], t3rs.at[r], (mx, gy_peer(r)))

    def t2_copy(r):
        return send(t2s.at[gx_peer(r)], t2r.at[mx], t2ss.at[r], t2rs.at[r], (gx_peer(r), my))

    def g2_copy(r):
        return send(g2s, g2r.at[mx], g2ss.at[r], g2rs.at[r], (gx_peer(r), my))

    def g3_copy(r):
        return send(g3s, g3r.at[my], g3ss.at[r], g3rs.at[r], (mx, gy_peer(r)))

    m1s[:, 1] = jnp.zeros((N, 4, 400), F32)
    for g in range(N):
        m1s[g, 0] = m1a[6 * g : 6 * g + 4]
        m1s[g, 1, 0:2] = m1a[6 * g + 4 : 6 * g + 6]
        t3s[g] = m3a[4 * g : 4 * g + 4]
        t2s[g] = m2a[g : g + 1]

    def first_exchange(r):
        t2_copy(r).start()
        t3_copy(r).start()

    each(1, N, first_exchange)
    t3r[my] = t3s[my]
    t2r[mx] = t2s[mx]
    ring(2)

    def field_arrives(r):
        f_copy(r).wait_recv()
        f_x(r).start()

    for r in (1, 15, 2, 14, 3, 13, 4, 12, 5, 11, 6, 10, 7, 9, 8):
        field_arrives(r)
    c2f[...] = jnp.zeros_like(c2f)
    for g in range(N):
        c2f[:, BLK * g : BLK * g + 50] = c2_ref[:, 50 * g : 50 * g + 50].astype(F32)
    c2all[four, xlo, core] = c2f[...].astype(BF16)
    c2_y.start()
    f_core.start()
    ring(3)
    c2_y.wait_recv()
    each(1, 4, lambda r: c2_x(r).start())

    row = lax.broadcasted_iota(jnp.int32, (64, 64), 0)
    hour = lax.broadcasted_iota(jnp.int32, (64, 64), 1)
    arranged = hour == 4 * (row & 15) + 2 * ((row >> 4) & 1) + (row >> 5)
    c3v[...] = jnp.dot(
        arranged.astype(BF16), c3_ref[...], preferred_element_type=F32
    ).astype(BF16)
    store[0].start()
    ring(4)

    each(1, N, lambda r: t3_copy(r).wait_recv())
    each(1, N, lambda r: t2_copy(r).wait_recv())
    three = jnp.sum(t3r[...], axis=0)
    for k in range(4):
        g2s[k] = three[k : k + 1]
    g2s[4] = jnp.sum(t2r[...], axis=0)
    each(1, N, lambda r: g2_copy(r).start())
    g2r[mx] = g2s[...]

    each(0, N, x_arrives)
    each(1, 4, lambda r: c2_x(r).wait_recv())
    c2_core.start()

    def total(side, wait):
        got = jnp.zeros((128, WIN), F32)
        for o in OFFSETS:
            for low in range(2):
                g = shard(o, (ylo + low) % 2)
                if low and wait:
                    y_copy(o, 0).wait_recv()
                    y_copy(o, 1).wait_recv()
                pair = fall[g, pl.ds(2 * side, 2)]
                three = [pair[:, k].reshape(32, 128) for k in range(3)]
                last = jnp.concatenate([three[k][:, 96:128] for k in range(3)], axis=1)
                rows = jnp.concatenate([three[k][:, 0:96] for k in range(3)] + [last], axis=0)
                got += jnp.dot(rows, cfall[g], preferred_element_type=F32)
        acct[side] = got.T

    f_core.wait_recv()
    total(xlo, True)
    each(0, N, lambda r: f_x_core(r).wait_recv())
    total(1 - xlo, False)

    def m_copy(m):
        return send(fms.at[m], fmr.at[four], p2s.at[m], p2r.at[four], (4 * quarter + m, mx))

    def stays(m):
        return jnp.logical_and(4 * quarter + m == mx, mx == my)

    for m in range(4):
        rows = slice(50 * m, 50 * m + BLK)
        fms[m] = jnp.concatenate([acct[0, rows], acct[1, rows]], axis=1).astype(BF16)

        @pl.when(jnp.logical_not(stays(m)))
        def _():
            m_copy(m).start()

        @pl.when(stays(m))
        def _():
            fmr[four] = fms[m]

    each(1, N, lambda r: m1_copy(r).start())
    m1r[my] = m1s[my]

    each(1, N, lambda r: g2_copy(r).wait_recv())
    g3s[...] = jnp.concatenate([jnp.sum(g2r[:, k], axis=0) for k in range(4)], axis=0)
    each(1, N, lambda r: g3_copy(r).start())
    g3r[my] = g3s[...]
    for g in range(N):
        twov[g : g + 1] = g2r[g, 4]
    store[2].start()
    c2_core.wait_recv()

    sent_quarter = mx // 4
    from_self = jnp.logical_and(mx == my, sent_quarter == quarter)

    def first_arrives(s):
        @pl.when(jnp.logical_not(jnp.logical_and(from_self, s == four)))
        def _():
            send(fms.at[0], fmr.at[s], p2s.at[0], p2r.at[s], other_core).wait_recv()

    each(0, 4, first_arrives)
    for s in range(4):
        part = fmr[s].astype(F32)
        for t in range(4):
            for side in range(2):
                to, at = BLK * s + 32 * side, 128 * side + 32 * t
                lhsf[BLK * t : BLK * t + BLK, to : to + 32] = part[:, at : at + 32]
    lhs = lhsf[...].astype(BF16)
    low_lanes = lax.broadcasted_iota(jnp.int32, (BLK, 128), 1) < BLK
    def p3_copy(g):
        return send(sms.at[g], rr.at[my], p3s.at[g], p3r.at[my], (mx, g))

    for ahead in (2, 1, 3, 0):
        u = lax.rem(x + ahead, 4)
        columns = pl.ds(pl.multiple_of(256 * u, 256), 256)
        rhs = c2all[:, :, :, :, columns].reshape(256, 256)
        got = jnp.dot(lhs, rhs, preferred_element_type=F32)
        for v in range(2):
            g = 4 * u + 2 * v
            lower, upper = [], []
            for p in range(2):
                tile = slice(128 * v, 128 * v + 128)
                first = got[2 * BLK * p : 2 * BLK * p + BLK, tile]
                second = got[2 * BLK * p + BLK : 2 * BLK * p + 2 * BLK, tile]
                lower.append(jnp.where(low_lanes, first, pltpu.roll(second, BLK, 1))[0:50])
                upper.append(jnp.where(low_lanes, pltpu.roll(first, BLK, 1), second)[0:50])
            fill = [jnp.zeros((ROWS - 100, 128), F32)]
            sms[g] = jnp.concatenate(lower + fill, axis=0).astype(BF16)
            sms[g + 1] = jnp.concatenate(upper + fill, axis=0).astype(BF16)
            for to in (g, g + 1):
                if ahead:
                    p3_copy(to).start()
                else:

                    @pl.when(to != my)
                    def _():
                        p3_copy(to).start()

    rr[my] = sms[my]

    each(1, N, lambda r: m1_copy(r).wait_recv())
    onev[0:4] = jnp.sum(m1r[:, 0], axis=0)
    onev[4:6] = jnp.sum(m1r[:, 1], axis=0)[0:2]
    store[1].start()
    each(1, N, lambda r: g3_copy(r).wait_recv())
    for g in range(N):
        threev[4 * g : 4 * g + 4] = g3r[g]
    store[3].start()

    for step in range(1, 5):
        z_copy(1, step).wait_send()
    for step in range(1, 4):
        z_copy(-1, step).wait_send()
    for o in OFFSETS:
        y_copy(o, 0).wait_send()
        y_copy(o, 1).wait_send()
    c2_y.wait_send()
    each(1, 4, lambda r: c2_x(r).wait_send())
    c2_core.wait_send()
    f_core.wait_send()
    f_x(0).wait_send()
    f_x_core(0).wait_send()

    def left(r):
        f_copy(r).wait_send()
        f_x(r).wait_send()
        f_x_core(r).wait_send()
        m1_copy(r).wait_send()
        t3_copy(r).wait_send()
        t2_copy(r).wait_send()
        g2_copy(r).wait_send()
        g3_copy(r).wait_send()

    each(1, N, left)
    for m in range(4):

        @pl.when(jnp.logical_not(stays(m)))
        def _():
            m_copy(m).wait_send()

    def second_arrives(r):
        send(sms.at[0], rr.at[0], p3s.at[0], p3r.at[gy_peer(r)], other_core).wait_recv()
        keep(gy_peer(r)).start()

    def keep(g):
        return pltpu.make_async_copy(rr.at[g], rr_out.at[g], keeps.at[g])

    keep(my).start()
    each(1, N, second_arrives)
    for one in store:
        one.wait()
    each(0, N, lambda g: keep(g).wait())
    each(1, N, lambda r: p3_copy(gy_peer(r)).wait_send())


CHUNKS = (3, 5, 8, 10, 12, 12)


def hours_kernel(
    rr_hbm, c3_hbm, m1_hbm, m2_hbm, m3_hbm, core_out, one_out, two_out, three_out,
    rr_ref, c3_ref, m1_ref, m2_ref, m3_ref, rrf, lhs, core_ref, loads, passes, stores,
):
    get_rr = pltpu.make_async_copy(rr_hbm, rr_ref, loads.at[0])
    get_c3 = pltpu.make_async_copy(c3_hbm, c3_ref, loads.at[1])
    get_rr.start()
    get_c3.start()
    modes = ((m1_hbm, m1_ref, one_out), (m2_hbm, m2_ref, two_out), (m3_hbm, m3_ref, three_out))
    taken = [pltpu.make_async_copy(a, b, passes.at[i]) for i, (a, b, _) in enumerate(modes)]
    passed = [pltpu.make_async_copy(b, c, passes.at[3 + i]) for i, (_, b, c) in enumerate(modes)]
    for one in taken:
        one.start()
    get_rr.wait()
    for g in range(N):
        rrf[ROWS * g : ROWS * g + ROWS, :] = rr_ref[g].astype(F32)
    get_c3.wait()
    for i in range(3):
        taken[i].wait()
        passed[i].start()

    stored, done = [], 0
    for i, chunk in enumerate(CHUNKS):
        for a in range(done, done + chunk):
            hours = [rrf[pl.ds(50 * p + a, N, stride=ROWS), :] for p in range(2)]
            turned = jnp.concatenate(hours, axis=0).T
            lhs[56 * a : 56 * a + 56, 0:32] = turned[0:56]
            lhs[56 * a : 56 * a + 56, 32:64] = turned[BLK : BLK + 56]
        got = jnp.dot(
            lhs[56 * done : 56 * (done + chunk)].astype(BF16), c3_ref[...],
            preferred_element_type=F32,
        )
        for k in range(chunk):
            core_ref[done + k] = got[56 * k : 56 * k + 50]
        rows = pl.ds(done, chunk)
        stored.append(pltpu.make_async_copy(core_ref.at[rows], core_out.at[rows], stores.at[i]))
        stored[-1].start()
        done += chunk
    for one in passed + stored:
        one.wait()


def on_device(
    field_slab, one_by_second, one_by_hours, two_by_first, two_by_hours,
    three_by_first, three_by_second, core_first, core_second, core_hours,
):
    hbm = pl.BlockSpec(memory_space=pltpu.HBM)
    dma = pltpu.SemaphoreType.DMA
    arguments = (
        jnp.transpose(field_slab, (1, 2, 0)), core_first.T, core_second.T, core_hours.T,
        one_by_second, one_by_hours, two_by_first, two_by_hours, three_by_first, three_by_second,
    )
    sizes = (
        ((N, ROWS, 128), BF16), ((64, 800), BF16), ((6, 400), F32), ((16, 400), F32), ((64, 400), F32)
    )
    ways = [10, 4, 16, 16, 16, 16, 16, 16, 16, 1, 1, 7, 7, 16, 16, 5, 5, 4, 4, 16, 16] + [16] * 10
    between = pl.pallas_call(
        exchange_kernel,
        out_shape=tuple(jax.ShapeDtypeStruct(shape, dtype) for shape, dtype in sizes),
        in_specs=[hbm] * 10,
        out_specs=(hbm,) * 5,
        scratch_shapes=[pltpu.VMEM(a.shape, a.dtype) for a in arguments]
        + [
            pltpu.VMEM((1024, 128), F32),
            pltpu.VMEM((N, 3, 16, 128), BF16),
            pltpu.VMEM((N, 4, 3, 16, 128), BF16),
            pltpu.VMEM((N, 96, WIN), BF16),
            pltpu.VMEM((16, 1024), F32),
            pltpu.VMEM((4, 2, 2, 16, 1024), BF16),
            pltpu.VMEM((16, 400), F32),
            pltpu.VMEM((16, 400), F32),
            pltpu.VMEM((2, WIN, 128), F32),
            pltpu.VMEM((4, BLK, 256), BF16),
            pltpu.VMEM((4, BLK, 256), BF16),
            pltpu.VMEM((256, 256), F32),
            pltpu.VMEM((N, ROWS, 128), BF16),
            pltpu.VMEM((N, ROWS, 128), BF16),
            pltpu.VMEM((64, 800), BF16),
            pltpu.VMEM((6, 400), F32),
            pltpu.VMEM((16, 400), F32),
            pltpu.VMEM((64, 400), F32),
            pltpu.VMEM((96, 400), F32),
            pltpu.VMEM((16, 400), F32),
            pltpu.VMEM((64, 400), F32),
            pltpu.VMEM((N, 2, 4, 400), F32),
            pltpu.VMEM((N, 2, 4, 400), F32),
            pltpu.VMEM((N, 4, 400), F32),
            pltpu.VMEM((N, 4, 400), F32),
            pltpu.VMEM((N, 1, 400), F32),
            pltpu.VMEM((N, 1, 400), F32),
            pltpu.VMEM((5, 1, 400), F32),
            pltpu.VMEM((N, 5, 1, 400), F32),
            pltpu.VMEM((4, 400), F32),
            pltpu.VMEM((N, 4, 400), F32),
        ]
        + [dma((n,)) for n in ways],
        compiler_params=pltpu.CompilerParams(
            collective_id=0, has_side_effects=True, vmem_limit_bytes=60 * 2**20
        ),
        cost_estimate=pl.CostEstimate(flops=500_000_000, bytes_accessed=2_000_000, transcendentals=0),
        name="exchange",
    )(*arguments)

    core_sketch, mode_one, mode_two, mode_three = pl.pallas_call(
        hours_kernel,
        out_shape=(
            jax.ShapeDtypeStruct((50, 50, 800), F32),
            jax.ShapeDtypeStruct((6, 400), F32),
            jax.ShapeDtypeStruct((16, 400), F32),
            jax.ShapeDtypeStruct((64, 400), F32),
        ),
        in_specs=[hbm] * 5,
        out_specs=(hbm,) * 4,
        scratch_shapes=[
            pltpu.VMEM((N, ROWS, 128), BF16),
            pltpu.VMEM((64, 800), BF16),
            pltpu.VMEM((6, 400), F32),
            pltpu.VMEM((16, 400), F32),
            pltpu.VMEM((64, 400), F32),
            pltpu.VMEM((N * ROWS, 128), F32),
            pltpu.VMEM((56 * 50, 64), F32),
            pltpu.VMEM((50, 50, 800), F32),
            dma((2,)), dma((6,)), dma((len(CHUNKS),)),
        ],
        compiler_params=pltpu.CompilerParams(vmem_limit_bytes=60 * 2**20),
        cost_estimate=pl.CostEstimate(flops=260_000_000, bytes_accessed=11_000_000, transcendentals=0),
        name="hours",
    )(*between)
    return mode_one, mode_two, mode_three, core_sketch


def solution(mesh):
    in_specs = (
        P("gx", "gy", None),
        P("gy", None),
        P(),
        P("gx", None),
        P(),
        P("gx", None),
        P("gy", None),
        P(None, "gx"),
        P(None, "gy"),
        P(),
    )
    out_specs = (P(("gx", "gy"), None), P("gy", None), P(), P("gx", "gy", None))
    return jax.shard_map(
        on_device, mesh=mesh, in_specs=in_specs, out_specs=out_specs, check_vma=False
    )
```
